256 devices in a mesh: ctx: 16 (over x_hi, y, core), head: 16 (over x_lo, z).
Axes of the slice: x: 4 (x_hi: 2, x_lo: 2; x = x_hi * 2 + x_lo), y: 4, z: 8, core: 2. Of those that a mesh axis runs over, the one named last changes fastest.
Arguments:
- q_nope: bfloat16 [2048, 16384], P('ctx', 'head'), may hold values from -6 to 6
- q_rope: bfloat16 [2048, 8192], P('ctx', 'head'), may hold values from -6 to 6
- compressed: bfloat16 [2048, 576], P('ctx'), may hold values from -6 to 6
- w_uk: bfloat16 [512, 16384], P(None, 'head'), may hold values from -0.25 to 0.25
- w_uv: bfloat16 [512, 16384], P(None, 'head'), may hold values from -0.25 to 0.25
- grad_out: bfloat16 [2048, 16384], P('ctx', 'head'), may hold values from -6 to 6
- positions: int32 [2048], P('ctx'), may hold values from 0 to 16383, as said below
- block_map: int32 [16, 2], replicated, may hold values from 0 to 31, as said below
Outputs:
- grad_q_nope: bfloat16 [2048, 16384], P('ctx', 'head')
- grad_q_rope: bfloat16 [2048, 8192], P('ctx', 'head')
- grad_compressed: bfloat16 [2048, 576], P('ctx')
The draws below stay inside these ranges and needn't reach their ends.
Inputs may be any that keep to these rules, and one draw needn't show every extreme that they name: Token rows r * 128 to (r + 1) * 128 - 1 hold block block_map[r, 0] followed by block block_map[r, 1] of the 32 blocks of 64 tokens; block_map[r, 1] = 31 - block_map[r, 0]; every block appears once. Within each block the positions rise by one from a start of their own.
All inputs are finite; a program needn't handle non-finite values.
Results may differ from the reference program's by a relative error of at most 0.034.
Values may be sent and summed in bfloat16 or wider, within the bound.
No kernel may reach another device: no remote copies, remote signals or barrier semaphores. Data moves between devices by JAX's collectives and lax.ppermute only.
A program may use at most 128 MiB of HBM per device.

```python
import math
import jax
import jax.numpy as jnp
from jax import lax

HEADS = 128
D_NOPE = 128
D_ROPE = 64
D_V = 128
D_LAT = 512
BLOCK = 64
TOKENS = 2048
N_CTX = 16


def draw_q_nope(key, part):
    key = jax.random.fold_in(key, 13)
    drawn = jnp.clip(jax.random.normal(key, (TOKENS, HEADS * D_NOPE), jnp.float32), -6.0, 6.0)
    return drawn.astype(jnp.bfloat16)


def draw_q_rope(key, part):
    key = jax.random.fold_in(key, 14)
    drawn = jnp.clip(jax.random.normal(key, (TOKENS, HEADS * D_ROPE), jnp.float32), -6.0, 6.0)
    return drawn.astype(jnp.bfloat16)


def draw_compressed(key, part):
    key = jax.random.fold_in(key, 15)
    drawn = jnp.clip(jax.random.normal(key, (TOKENS, D_LAT + D_ROPE), jnp.float32), -6.0, 6.0)
    return drawn.astype(jnp.bfloat16)


def draw_block_map(key, part):
    key = jax.random.fold_in(key, 11)
    first = jax.random.permutation(key, N_CTX).astype(jnp.int32)
    return jnp.stack([first, 2 * N_CTX - 1 - first], axis=1)


def draw_positions(key, part):
    key = jax.random.fold_in(key, 12)
    starts = jax.random.randint(key, (N_CTX * 2, 1), 0, 16384 - BLOCK + 1, dtype=jnp.int32)
    starts = starts.at[0, 0].set(0)
    starts = starts.at[1, 0].set(16384 - BLOCK)
    return (starts + jnp.arange(BLOCK, dtype=jnp.int32)[None, :]).reshape(-1)


def shard_levels(stream_key, shape, split, low, largest):
    def one(axis_at, shards_of):
        steps = jax.random.uniform(jax.random.fold_in(jax.random.fold_in(stream_key, 6), axis_at), (shards_of,), jnp.float32, low / len(split), largest / len(split))
        return jnp.repeat(jnp.exp(steps), shape[axis_at] // shards_of).reshape((-1,) + (1,) * (len(shape) - axis_at - 1))

    level = one(*split[0])
    for cut in split[1:]:
        level = level * one(*cut)
    return level


def normal_values(rng, dims, deviation, limit, split=(), kind=jnp.bfloat16):
    gain = shard_levels(rng, dims, split, -0.22, 0.18) if split else 1.0
    entries = jax.random.normal(rng, dims, jnp.float32) * deviation * gain
    return jnp.minimum(jnp.maximum(entries, -limit), limit).astype(kind)


def setup_inputs(seed: int = 0) -> dict:
    key_of = jax.random.split(jax.random.key(seed), 9)
    q_nope = draw_q_nope(jax.random.fold_in(key_of[8], 71), 0)
    q_rope = draw_q_rope(jax.random.fold_in(key_of[8], 71), 0)
    compressed = draw_compressed(jax.random.fold_in(key_of[8], 71), 0)
    w_uk = normal_values(key_of[3], (D_LAT, HEADS * D_NOPE), D_LAT ** -0.5, 0.25, ((1, 16),))
    w_uv = normal_values(key_of[4], (D_LAT, HEADS * D_V), D_LAT ** -0.5, 0.25, ((1, 16),))
    grad_out = normal_values(key_of[5], (TOKENS, HEADS * D_V), 1.0, 6.0, ((0, 16), (1, 16)))
    positions = draw_positions(jax.random.fold_in(key_of[8], 71), 0)
    block_map = draw_block_map(jax.random.fold_in(key_of[8], 71), 0)
    return dict(q_nope=q_nope, q_rope=q_rope, compressed=compressed, w_uk=w_uk, w_uv=w_uv, grad_out=grad_out, positions=positions, block_map=block_map)


attn_boost = (0.1 * math.log(40.0) + 1.0) ** 2


def yarn_freqs(half):
    index = jnp.arange(half, dtype=jnp.float32)
    width = 2 * half
    extra = jnp.power(10000.0, -2.0 * index / width)
    inter = extra / 40.0
    lower = math.floor(width * math.log(4096.0 / (32.0 * 2.0 * math.pi)) / (2.0 * math.log(10000.0)))
    upper = math.ceil(width * math.log(4096.0 / (1.0 * 2.0 * math.pi)) / (2.0 * math.log(10000.0)))
    lower = max(lower, 0)
    upper = min(upper, half - 1)
    spread = max(upper - lower, 0.001)
    ramp = jnp.clip((index - lower) / spread, 0.0, 1.0)
    return inter * ramp + extra * (1.0 - ramp)


def angles(positions, half):
    turn = positions.astype(jnp.float32)[:, None] * yarn_freqs(half)[None, :]
    return jnp.cos(turn), jnp.sin(turn)


def rotate(values, cosine, sine):
    half = values.shape[-1] // 2
    first, second = values[..., :half], values[..., half:]
    return jnp.concatenate([first * cosine - second * sine, second * cosine + first * sine], axis=-1)


def unrotate(grads, cosine, sine):
    half = grads.shape[-1] // 2
    first, second = grads[..., :half], grads[..., half:]
    return jnp.concatenate([first * cosine + second * sine, second * cosine - first * sine], axis=-1)


def reference(q_nope, q_rope, compressed, w_uk, w_uv, grad_out, positions, block_map):
    total = q_nope.shape[0]
    cosine, sine = angles(positions, D_ROPE // 2)
    blocks = jnp.repeat(block_map.reshape(-1), BLOCK, total_repeat_length=total)
    order = blocks * BLOCK + jnp.arange(total, dtype=jnp.int32) % BLOCK
    latent = compressed[:, :D_LAT]
    k_rot = rotate(compressed[:, D_LAT:].astype(jnp.float32), cosine, sine).astype(jnp.bfloat16)
    keys = jnp.dot(latent, w_uk, preferred_element_type=jnp.float32).astype(jnp.bfloat16)
    keys = keys.reshape(total, HEADS, D_NOPE).transpose(1, 0, 2)
    values = jnp.dot(latent, w_uv, preferred_element_type=jnp.float32).astype(jnp.bfloat16)
    values = values.reshape(total, HEADS, D_V).transpose(1, 0, 2)
    query_plain = q_nope.reshape(total, HEADS, D_NOPE).transpose(1, 0, 2)
    query_rot = rotate(q_rope.reshape(total, HEADS, D_ROPE).astype(jnp.float32), cosine[:, None, :], sine[:, None, :])
    query_rot = query_rot.astype(jnp.bfloat16).transpose(1, 0, 2)
    cotangent = grad_out.reshape(total, HEADS, D_V).transpose(1, 0, 2)
    allowed = order[None, :] <= order[:, None]
    scale = (D_NOPE + D_ROPE) ** -0.5 * attn_boost

    def one_head(items):
        plain_h, rot_h, key_h, value_h, cot_h = items
        scores = jnp.dot(plain_h, key_h.T, preferred_element_type=jnp.float32)
        scores = (scores + jnp.dot(rot_h, k_rot.T, preferred_element_type=jnp.float32)) * scale
        scores = jnp.where(allowed, scores, -1e30)
        top = jnp.max(scores, axis=1, keepdims=True)
        lse = top + jnp.log(jnp.sum(jnp.exp(scores - top), axis=1, keepdims=True))
        probs = jnp.exp(scores - lse).astype(jnp.bfloat16)
        dprobs = jnp.dot(cot_h, value_h.T, preferred_element_type=jnp.float32)
        delta = jnp.sum(probs.astype(jnp.float32) * dprobs, axis=1, keepdims=True)
        dscores = (probs.astype(jnp.float32) * (dprobs - delta) * scale).astype(jnp.bfloat16)
        return (jnp.dot(dscores, key_h, preferred_element_type=jnp.float32),
                jnp.dot(dscores, k_rot, preferred_element_type=jnp.float32),
                jnp.dot(dscores.T, plain_h, preferred_element_type=jnp.float32),
                jnp.dot(probs.T, cot_h, preferred_element_type=jnp.float32),
                jnp.dot(dscores.T, rot_h, preferred_element_type=jnp.float32))

    dplain, drot, dkeys, dvalues, dkrot = lax.map(one_head, (query_plain, query_rot, keys, values, cotangent))
    grad_q_nope = dplain.transpose(1, 0, 2).reshape(total, HEADS * D_NOPE).astype(jnp.bfloat16)
    grad_q_rope = unrotate(drot.transpose(1, 0, 2), cosine[:, None, :], sine[:, None, :])
    grad_q_rope = grad_q_rope.reshape(total, HEADS * D_ROPE).astype(jnp.bfloat16)
    dkeys = dkeys.transpose(1, 0, 2).reshape(total, HEADS * D_NOPE)
    dvalues = dvalues.transpose(1, 0, 2).reshape(total, HEADS * D_V)
    grad_latent = jnp.dot(dkeys, w_uk.astype(jnp.float32).T, precision=lax.Precision.HIGHEST)
    grad_latent = grad_latent + jnp.dot(dvalues, w_uv.astype(jnp.float32).T, precision=lax.Precision.HIGHEST)
    grad_shared = unrotate(jnp.sum(dkrot, axis=0), cosine, sine)
    grad_compressed = jnp.concatenate([grad_latent, grad_shared], axis=1).astype(jnp.bfloat16)
    return grad_q_nope, grad_q_rope, grad_compressed
```

```python
import math

import jax
import jax.numpy as jnp
import numpy as np
from jax import lax
from jax.experimental import pallas as pl
from jax.experimental.pallas import tpu as pltpu
from jax.sharding import PartitionSpec as P

D_NOPE = 128
D_ROPE = 64
D_V = 128
D_LAT = 512
D_ALL = D_LAT + D_ROPE
N_CTX = 16
N_CHIP = 8
N_HEAD = 16
ROWS = 128
HALF = 64
TOTAL = ROWS * N_CTX
HEADS = 8
LANES = HEADS * HALF
CHUNK = 256
N_CHUNK = TOTAL // CHUNK
PER_CHUNK = CHUNK // HALF
N_BLOCK = TOTAL // HALF

SCALE = (D_NOPE + D_ROPE) ** (-0.5) * (0.1 * math.log(40.0) + 1.0) ** 2
LOG2E = math.log2(math.e)
HIDDEN = -1e30
CORES = [[c for c in range(N_CTX) if c % 2 == k] for k in range(2)]
SWAP = [(c, c ^ 1) for c in range(N_CTX)]

bf16 = jnp.bfloat16
f32 = jnp.float32


def frequencies():
    half = D_ROPE // 2
    index = np.arange(half, dtype=np.float64)
    width = 2 * half
    extra = np.power(10000.0, -2.0 * index / width)
    inter = extra / 40.0
    lower = math.floor(width * math.log(4096.0 / (32.0 * 2.0 * math.pi)) / (2.0 * math.log(10000.0)))
    upper = math.ceil(width * math.log(4096.0 / (1.0 * 2.0 * math.pi)) / (2.0 * math.log(10000.0)))
    lower = max(lower, 0)
    upper = min(upper, half - 1)
    spread = max(upper - lower, 0.001)
    ramp = np.clip((index - lower) / spread, 0.0, 1.0)
    inv = inter * ramp + extra * (1.0 - ramp)
    return np.tile(inv, 4).astype(np.float32)[None, :]


def split_half_pi():
    rest = math.pi / 2
    parts = []
    for bits in (9, 19):
        part = math.floor(rest * 2.0**bits) / 2.0**bits
        parts.append(part)
        rest -= part
    return parts + [rest]


HALF_PI = split_half_pi()


def cos_sin(angle):
    turns = jnp.floor(angle * (2.0 / math.pi) + 0.5)
    r = angle - turns * HALF_PI[0]
    r = r - turns * HALF_PI[1]
    r = r - turns * HALF_PI[2]
    r2 = r * r
    sine = r + r * r2 * (-1.0 / 6 + r2 * (1.0 / 120 + r2 * (-1.0 / 5040 + r2 * (1.0 / 362880))))
    cosine = 1.0 + r2 * (-0.5 + r2 * (1.0 / 24 + r2 * (-1.0 / 720 + r2 * (1.0 / 40320))))
    quarter = turns.astype(jnp.int32) & 3
    odd = (quarter & 1) == 1
    cos_out = jnp.where(odd, sine, cosine)
    sin_out = jnp.where(odd, cosine, sine)
    cos_out = jnp.where((quarter == 1) | (quarter == 2), -cos_out, cos_out)
    sin_out = jnp.where(quarter >= 2, -sin_out, sin_out)
    return cos_out, sin_out


def lanes_of(shape):
    return lax.broadcasted_iota(jnp.int32, shape, 1)


def swap_halves(x):
    return jnp.where((lanes_of(x.shape) & 63) < 32, pltpu.roll(x, 96, 1), pltpu.roll(x, 32, 1))


def pair_tile(first, second, half):
    low = lanes_of(first.shape) < HALF
    if half == 0:
        return jnp.where(low, first, pltpu.roll(second, HALF, 1))
    return jnp.where(low, pltpu.roll(first, HALF, 1), second)


def share_kernel(pos_ref, inv_ref, comp_ref, out_ref, cos_ref, sin_ref):
    pos = jnp.broadcast_to(pos_ref[...].astype(f32), (ROWS, ROWS)).T
    cosine, sine = cos_sin(pos * inv_ref[...])
    sine = jnp.where((lanes_of(sine.shape) & 63) < 32, -sine, sine)
    cos_ref[...] = cosine
    sin_ref[...] = sine
    x = comp_ref[:, D_LAT:].astype(f32)
    x = jnp.concatenate([x, x], axis=1)
    rotated = (x * cosine + pltpu.roll(x, 32, 1) * sine)[:, :D_ROPE].astype(bf16)
    latent = comp_ref[:, :D_LAT]
    for i in range(N_CHIP):
        out_ref[i, :, :D_LAT] = latent
        out_ref[i, :, D_LAT:] = rotated


def absorb_kernel(qn_ref, qr_ref, go_ref, uk_ref, uv_ref, cos_ref, sin_ref,
                  qt_ref, qa_ref, gt_ref, ga_ref, tall):
    contract = (((1,), (1,)), ((), ()))
    x = qr_ref[...].astype(f32)
    rotated = x * cos_ref[...] + swap_halves(x) * sin_ref[...]
    turned = pltpu.roll(rotated, HALF, 1)
    for h in range(2):
        cols = slice(h * D_NOPE, (h + 1) * D_NOPE)
        q = lax.dot_general(qn_ref[:, cols], uk_ref[:, cols], contract, preferred_element_type=f32)
        g = lax.dot_general(go_ref[:, cols], uv_ref[:, cols], contract, preferred_element_type=f32)
        rope = rotated if h == 0 else turned
        for j in range(2):
            src = slice(j * HALF, (j + 1) * HALF)
            dst = slice(h * HALF, (h + 1) * HALF)
            tall[j, dst, :D_LAT] = q[src]
            tall[j, dst, D_LAT:D_LAT + 128] = rope[src]
            tall[j, dst, D_LAT + 128:] = g[src]
    for j in range(2):
        both = tall[j, :, :D_LAT + 128]
        qa_ref[j] = (both[:, :D_ALL] * SCALE).astype(bf16)
        ga_ref[j] = tall[j, :, D_LAT + 128:].astype(bf16)
        for k in range(4):
            piece = slice(k * 128, (k + 1) * 128)
            qt_ref[j, piece, :] = (both[:, piece] * (SCALE * LOG2E)).T.astype(bf16)
            gt_ref[j, piece, :] = tall[j, :, D_LAT + 128 + k * 128:D_LAT + 256 + k * 128].T.astype(bf16)
        qt_ref[j, D_LAT:, :] = (both[:, D_LAT:] * (SCALE * LOG2E)).T[:D_ROPE].astype(bf16)


def sort_copies(bm_ref, core, mine_ref, other_ref, keys, sems):
    for chip in range(N_CHIP):
        for j in range(2):
            for k, ref in enumerate((mine_ref, other_ref)):
                row = 2 * chip + (core ^ k)
                block = bm_ref[row, j]
                yield pltpu.make_async_copy(
                    ref.at[chip, pl.ds(j * HALF, HALF)],
                    keys.at[pl.ds(pl.multiple_of(block * HALF, HALF), HALF)],
                    sems.at[(chip * 2 + j) * 2 + k],
                )


def attend_kernel(bm_ref, rank_ref, mine_ref, other_ref, qt_hbm, qa_hbm, gt_hbm, ga_hbm,
                  dmine_ref, dother_ref, ds_hbm,
                  keys, qt, qa, gt, ga, probs, dprobs, tops, dlat, dlat_out, ds, place,
                  key_sems, load_sems, out_sems, ds_sems):
    rank = rank_ref[0]
    core = rank & 1
    loads = [
        pltpu.make_async_copy(src, dst, load_sems.at[i])
        for i, (src, dst) in enumerate(((qt_hbm, qt), (gt_hbm, gt), (qa_hbm, qa), (ga_hbm, ga)))
    ]
    copies = list(sort_copies(bm_ref, core, mine_ref, other_ref, keys, key_sems))
    loads[0].start()
    for copy in copies:
        copy.start()
    for load in loads[1:]:
        load.start()
    for row in range(N_CTX):
        for j in range(2):
            place[bm_ref[row, j]] = row * 2 + j
    dlat[...] = jnp.zeros_like(dlat)
    loads[0].wait()
    for copy in copies:
        copy.wait()
    loads[1].wait()

    first, second = bm_ref[rank, 0], bm_ref[rank, 1]
    low_j = jnp.where(first < second, 0, 1)
    low, high = jnp.minimum(first, second), jnp.maximum(first, second)

    def half_pass(j, block, emit):
        count = (block + PER_CHUNK) // PER_CHUNK

        def scores_step(c, carry):
            top, total, weighted = carry
            rows = pl.ds(pl.multiple_of(c * CHUNK, CHUNK), CHUNK)
            scores = jnp.dot(keys[rows, :], qt[j], preferred_element_type=f32)
            dp = jnp.dot(keys[rows, :D_LAT], gt[j], preferred_element_type=f32)
            key_at = lax.broadcasted_iota(jnp.int32, (CHUNK, LANES), 0) + c * CHUNK
            query_at = (lax.broadcasted_iota(jnp.int32, (CHUNK, LANES), 1) & (HALF - 1)) + block * HALF
            scores = jnp.where(key_at <= query_at, scores, HIDDEN)
            new_top = jnp.maximum(top, jnp.max(scores, axis=0, keepdims=True))
            e = jnp.exp2(scores - new_top)
            keep = jnp.exp2(top - new_top)
            probs[rows, :] = e
            dprobs[rows, :] = dp
            tops[c] = new_top
            total = total * keep + jnp.sum(e, axis=0, keepdims=True)
            weighted = weighted * keep + jnp.sum(e * dp, axis=0, keepdims=True)
            return new_top, total, weighted

        zero = jnp.zeros((1, LANES), f32)
        top, total, weighted = lax.fori_loop(
            0, count, scores_step, (jnp.full((1, LANES), HIDDEN, f32), zero, zero)
        )
        inverse = 1.0 / total
        delta = weighted * inverse

        def grads_step(c, carry):
            rows = pl.ds(pl.multiple_of(c * CHUNK, CHUNK), CHUNK)
            factor = jnp.exp2(tops[c] - top) * inverse
            p = probs[rows, :] * factor
            d = (p * (dprobs[rows, :] - delta)).astype(bf16)
            ds[j, rows, :] = d
            pltpu.make_async_copy(ds.at[j, rows], ds_hbm.at[j, rows], ds_sems.at[j, c]).start()
            part = jnp.dot(d, qa[j], preferred_element_type=f32)
            values = jnp.dot(p.astype(bf16), ga[j], preferred_element_type=f32)
            if emit is None:
                dlat[rows, :D_LAT] = part[:, :D_LAT] + values
                dlat[rows, D_LAT:] = part[:, D_LAT:]
            else:
                dlat_out[rows, :D_LAT] = (dlat[rows, :D_LAT] + part[:, :D_LAT] + values).astype(bf16)
                dlat_out[rows, D_LAT:] = (dlat[rows, D_LAT:] + part[:, D_LAT:]).astype(bf16)
                emit(c)
            return carry

        return count, grads_step

    def emit(c):
        for i in range(PER_CHUNK):
            block = c * PER_CHUNK + i
            src = dlat_out.at[pl.ds(pl.multiple_of(block * HALF, HALF), HALF)]
            at = place[block]
            row = at // 2
            rows = pl.ds(pl.multiple_of((at & 1) * HALF, HALF), HALF)
            ours = (row & 1) == core

            @pl.when(ours)
            def _():
                pltpu.make_async_copy(src, dmine_ref.at[row // 2, rows], out_sems.at[block]).start()

            @pl.when(jnp.logical_not(ours))
            def _():
                pltpu.make_async_copy(src, dother_ref.at[row // 2, rows], out_sems.at[block]).start()

    low_count, low_step = half_pass(low_j, low, None)
    loads[2].wait()
    loads[3].wait()
    lax.fori_loop(0, low_count, low_step, 0)
    high_count, high_step = half_pass(1 - low_j, high, emit)
    lax.fori_loop(0, high_count, high_step, 0)

    def blank_step(c, carry):
        dlat_out[pl.ds(pl.multiple_of(c * CHUNK, CHUNK), CHUNK), :] = jnp.zeros((CHUNK, D_ALL), bf16)
        emit(c)
        return carry

    lax.fori_loop(high_count, N_CHUNK, blank_step, 0)

    for block in range(N_BLOCK):
        pltpu.make_async_copy(
            dlat_out.at[pl.ds(block * HALF, HALF)], dmine_ref.at[0, pl.ds(0, HALF)], out_sems.at[block]
        ).wait()
    for j, count in ((low_j, low_count), (1 - low_j, high_count)):
        def wait_step(c, carry):
            rows = pl.ds(pl.multiple_of(c * CHUNK, CHUNK), CHUNK)
            pltpu.make_async_copy(ds.at[j, rows], ds_hbm.at[j, rows], ds_sems.at[j, c]).wait()
            return carry

        lax.fori_loop(0, count, wait_step, 0)


def queries_kernel(bm_ref, rank_ref, mine_ref, other_ref, ds_hbm, uk_ref, cos_ref, sin_ref,
                   gqn_ref, gqr_ref, keys, ds, total, key_sems, ds_sems):
    rank = rank_ref[0]
    copies = list(sort_copies(bm_ref, rank & 1, mine_ref, other_ref, keys, key_sems))
    for copy in copies:
        copy.start()

    def moves(j, c):
        rows = pl.ds(pl.multiple_of(c * CHUNK, CHUNK), CHUNK)
        return pltpu.make_async_copy(ds_hbm.at[j, rows], ds.at[j, rows], ds_sems.at[j, c])

    counts = [(bm_ref[rank, j] + PER_CHUNK) // PER_CHUNK for j in range(2)]
    for j in range(2):
        def start_step(c, carry):
            moves(j, c).start()
            return carry

        lax.fori_loop(0, counts[j], start_step, 0)
    for copy in copies:
        copy.wait()
    total[...] = jnp.zeros_like(total)
    for j in range(2):
        def step(c, carry):
            rows = pl.ds(pl.multiple_of(c * CHUNK, CHUNK), CHUNK)
            moves(j, c).wait()
            total[j] += lax.dot_general(
                ds[j, rows, :], keys[rows, :], (((0,), (0,)), ((), ())), preferred_element_type=f32
            )
            return carry

        lax.fori_loop(0, counts[j], step, 0)
    for pair in range(HEADS // 2):
        ropes = []
        for h in (2 * pair, 2 * pair + 1):
            rows = slice(h * HALF, (h + 1) * HALF)
            both = jnp.concatenate([total[0, rows, :], total[1, rows, :]], axis=0) * SCALE
            cols = slice(h * D_NOPE, (h + 1) * D_NOPE)
            gqn_ref[:, cols] = jnp.dot(
                both[:, :D_LAT].astype(bf16), uk_ref[:, cols], preferred_element_type=f32
            ).astype(bf16)
            ropes.append(both[:, D_LAT:])
        g = jnp.concatenate(ropes, axis=1)
        g = g * cos_ref[...] - swap_halves(g) * sin_ref[...]
        gqr_ref[:, pair * 128:(pair + 1) * 128] = g.astype(bf16)


def chips_kernel(parts_ref, cos_ref, sin_ref, out_ref):
    total = parts_ref[0].astype(f32)
    for i in range(1, N_CHIP):
        total = total + parts_ref[i].astype(f32)
    out_ref[:, :D_LAT] = total[:, :D_LAT].astype(bf16)
    g = total[:, D_LAT:]
    g = jnp.concatenate([g, g], axis=1)
    g = g * cos_ref[...] - pltpu.roll(g, 32, 1) * sin_ref[...]
    out_ref[:, D_LAT:] = g[:, :D_ROPE].astype(bf16)


def heads_kernel(parts_ref, out_ref):
    total = parts_ref[0].astype(f32)
    for i in range(1, N_HEAD):
        total = total + parts_ref[i].astype(f32)
    total = total.astype(bf16)
    for i in range(N_HEAD):
        out_ref[i] = total


def whole(count):
    return [pl.BlockSpec(memory_space=pltpu.VMEM)] * count


def params(mib):
    return pltpu.CompilerParams(vmem_limit_bytes=mib * 1024 * 1024)


ANY = pl.BlockSpec(memory_space=pl.ANY)
SMEM = pl.BlockSpec(memory_space=pltpu.SMEM)


def on_device(q_nope, q_rope, compressed, w_uk, w_uv, grad_out, positions, block_map):
    rank = lax.axis_index("ctx").astype(jnp.int32).reshape(1)
    shape = jax.ShapeDtypeStruct
    table = shape((ROWS, 128), f32)
    shared, cosine, sine = pl.pallas_call(
        share_kernel,
        in_specs=whole(3),
        out_specs=tuple(whole(3)),
        out_shape=(shape((N_CHIP, ROWS, D_ALL), bf16), table, table),
        name="share",
    )(positions.reshape(1, ROWS), jnp.asarray(frequencies()), compressed)
    mine = lax.all_to_all(shared, "ctx", 0, 0, axis_index_groups=CORES)
    other = lax.ppermute(mine, "ctx", SWAP)

    pair_cols = lambda width: pl.BlockSpec((ROWS, width), lambda p: (0, p))
    fixed = pl.BlockSpec((ROWS, 128), lambda p: (0, 0))
    weight = pl.BlockSpec((D_LAT, 256), lambda p: (0, p))
    wide = lambda rows: pl.BlockSpec((2, rows, 128), lambda p: (0, 0, p))
    tall = lambda cols: pl.BlockSpec((2, 128, cols), lambda p: (0, p, 0))
    qt, qa, gt, ga = pl.pallas_call(
        absorb_kernel,
        grid=(HEADS // 2,),
        in_specs=[pair_cols(256), pair_cols(128), pair_cols(256), weight, weight, fixed, fixed],
        out_specs=(wide(D_ALL), tall(D_ALL), wide(D_LAT), tall(D_LAT)),
        out_shape=(
            shape((2, D_ALL, LANES), bf16),
            shape((2, LANES, D_ALL), bf16),
            shape((2, D_LAT, LANES), bf16),
            shape((2, LANES, D_LAT), bf16),
        ),
        scratch_shapes=[pltpu.VMEM((2, 128, 2 * D_LAT + 128), f32)],
        compiler_params=params(32),
        cost_estimate=pl.CostEstimate(flops=300_000_000, bytes_accessed=8_000_000, transcendentals=0),
        name="absorb",
    )(q_nope, q_rope, grad_out, w_uk, w_uv, cosine, sine)

    piece = shape((N_CHIP, ROWS, D_ALL), bf16)
    dma = pltpu.SemaphoreType.DMA
    dmine, dother, ds = pl.pallas_call(
        attend_kernel,
        in_specs=[SMEM, SMEM] + [ANY] * 6,
        out_specs=(ANY, ANY, ANY),
        out_shape=(piece, piece, shape((2, TOTAL, LANES), bf16)),
        scratch_shapes=[
            pltpu.VMEM((TOTAL, D_ALL), bf16),
            pltpu.VMEM((2, D_ALL, LANES), bf16),
            pltpu.VMEM((2, LANES, D_ALL), bf16),
            pltpu.VMEM((2, D_LAT, LANES), bf16),
            pltpu.VMEM((2, LANES, D_LAT), bf16),
            pltpu.VMEM((TOTAL, LANES), f32),
            pltpu.VMEM((TOTAL, LANES), f32),
            pltpu.VMEM((N_CHUNK, 1, LANES), f32),
            pltpu.VMEM((TOTAL, D_ALL), f32),
            pltpu.VMEM((TOTAL, D_ALL), bf16),
            pltpu.VMEM((2, TOTAL, LANES), bf16),
            pltpu.SMEM((N_BLOCK,), jnp.int32),
            dma((N_BLOCK,)),
            dma((4,)),
            dma((N_BLOCK,)),
            dma((2, N_CHUNK)),
        ],
        compiler_params=params(48),
        name="attend",
    )(block_map, rank, mine, other, qt, qa, gt, ga)

    theirs = lax.ppermute(dother, "ctx", SWAP)
    summed = (dmine.astype(f32) + theirs.astype(f32)).astype(bf16)
    parts = lax.all_to_all(summed, "ctx", 0, 0, axis_index_groups=CORES)

    grad_q_nope, grad_q_rope = pl.pallas_call(
        queries_kernel,
        in_specs=[SMEM, SMEM] + [ANY] * 3 + whole(3),
        out_specs=tuple(whole(2)),
        out_shape=(shape((ROWS, HEADS * D_NOPE), bf16), shape((ROWS, HEADS * D_ROPE), bf16)),
        scratch_shapes=[
            pltpu.VMEM((TOTAL, D_ALL), bf16),
            pltpu.VMEM((2, TOTAL, LANES), bf16),
            pltpu.VMEM((2, LANES, D_ALL), f32),
            dma((N_BLOCK,)),
            dma((2, N_CHUNK)),
        ],
        compiler_params=params(32),
        cost_estimate=pl.CostEstimate(flops=4_000_000_000, bytes_accessed=9_000_000, transcendentals=0),
        name="queries",
    )(block_map, rank, mine, other, ds, w_uk, cosine, sine)

    owned = pl.pallas_call(
        chips_kernel,
        in_specs=whole(3),
        out_specs=whole(1)[0],
        out_shape=shape((ROWS, D_ALL), bf16),
        name="chips",
    )(parts, cosine, sine)
    slabs = lax.all_to_all(owned.reshape(N_HEAD, ROWS // N_HEAD, D_ALL), "head", 0, 0)
    slabs = pl.pallas_call(
        heads_kernel,
        in_specs=whole(1),
        out_specs=whole(1)[0],
        out_shape=shape((N_HEAD, ROWS // N_HEAD, D_ALL), bf16),
        name="heads",
    )(slabs)
    grad_compressed = lax.all_to_all(slabs, "head", 0, 0).reshape(ROWS, D_ALL)
    return grad_q_nope, grad_q_rope, grad_compressed


def solution(mesh):
    in_specs = (
        P("ctx", "head"),
        P("ctx", "head"),
        P("ctx", None),
        P(None, "head"),
        P(None, "head"),
        P("ctx", "head"),
        P("ctx"),
        P(),
    )
    out_specs = (P("ctx", "head"), P("ctx", "head"), P("ctx", None))
    return jax.shard_map(
        on_device, mesh=mesh, in_specs=in_specs, out_specs=out_specs, check_vma=False
    )
```

```python
import math

import jax
import jax.numpy as jnp
import numpy as np
from jax import lax
from jax.experimental import pallas as pl
from jax.experimental.pallas import tpu as pltpu
from jax.sharding import PartitionSpec as P

D_NOPE = 128
D_ROPE = 64
D_V = 128
D_LAT = 512
D_ALL = D_LAT + D_ROPE
D_PAD = D_LAT + 128
PACKED = 144
N_CTX = 16
N_CHIP = 8
N_HEAD = 16
ROWS = 128
HALF = 64
TOTAL = ROWS * N_CTX
HEADS = 8
LANES = HEADS * HALF
CHUNK = 256
N_CHUNK = TOTAL // CHUNK
PER_CHUNK = CHUNK // HALF
N_BLOCK = TOTAL // HALF
STEPS = N_CHUNK + 1

SCALE = (D_NOPE + D_ROPE) ** (-0.5) * (0.1 * math.log(40.0) + 1.0) ** 2
LOG2E = math.log2(math.e)
HIDDEN = -1e30

GROUPS = [
    [c * N_HEAD + ((c // 8) ^ side) * 8 + z for c in range(core, N_CTX, 2)]
    for core in range(2)
    for side in range(2)
    for z in range(8)
]
SWAP = [(c, c ^ 1) for c in range(N_CTX)]

bf16 = jnp.bfloat16
f32 = jnp.float32


def frequencies():
    half = D_ROPE // 2
    index = np.arange(half, dtype=np.float64)
    width = 2 * half
    extra = np.power(10000.0, -2.0 * index / width)
    inter = extra / 40.0
    lower = math.floor(width * math.log(4096.0 / (32.0 * 2.0 * math.pi)) / (2.0 * math.log(10000.0)))
    upper = math.ceil(width * math.log(4096.0 / (1.0 * 2.0 * math.pi)) / (2.0 * math.log(10000.0)))
    lower = max(lower, 0)
    upper = min(upper, half - 1)
    spread = max(upper - lower, 0.001)
    ramp = np.clip((index - lower) / spread, 0.0, 1.0)
    inv = inter * ramp + extra * (1.0 - ramp)
    return np.tile(inv, 4).astype(np.float32)[None, :]


def split_half_pi():
    rest = math.pi / 2
    parts = []
    for bits in (9, 19):
        part = math.floor(rest * 2.0**bits) / 2.0**bits
        parts.append(part)
        rest -= part
    return parts + [rest]


HALF_PI = split_half_pi()


def cos_sin(angle):
    turns = jnp.floor(angle * (2.0 / math.pi) + 0.5)
    r = angle - turns * HALF_PI[0]
    r = r - turns * HALF_PI[1]
    r = r - turns * HALF_PI[2]
    r2 = r * r
    sine = r + r * r2 * (-1.0 / 6 + r2 * (1.0 / 120 + r2 * (-1.0 / 5040 + r2 * (1.0 / 362880))))
    cosine = 1.0 + r2 * (-0.5 + r2 * (1.0 / 24 + r2 * (-1.0 / 720 + r2 * (1.0 / 40320))))
    quarter = turns.astype(jnp.int32) & 3
    odd = (quarter & 1) == 1
    cos_out = jnp.where(odd, sine, cosine)
    sin_out = jnp.where(odd, cosine, sine)
    cos_out = jnp.where((quarter == 1) | (quarter == 2), -cos_out, cos_out)
    sin_out = jnp.where(quarter >= 2, -sin_out, sin_out)
    return cos_out, sin_out


def lanes_of(shape):
    return lax.broadcasted_iota(jnp.int32, shape, 1)


def swap_halves(x):
    return jnp.where((lanes_of(x.shape) & 63) < 32, pltpu.roll(x, 96, 1), pltpu.roll(x, 32, 1))


def pair_tile(first, second, half):
    low = lanes_of(first.shape) < HALF
    if half == 0:
        return jnp.where(low, first, pltpu.roll(second, HALF, 1))
    return jnp.where(low, pltpu.roll(first, HALF, 1), second)


def pack_rope(rope):
    low = lanes_of((16, 128)) < D_ROPE
    tiles = []
    for m in (0, 2):
        tiles.append(jnp.where(low, rope[16 * m:16 * m + 16], pltpu.roll(rope[16 * m + 16:16 * m + 32], D_ROPE, 1)))
    return jnp.concatenate(tiles, axis=1)


def unpack_rope(packed):
    low = lanes_of((16, 128)) < D_ROPE
    pieces = []
    for m in range(4):
        tile = packed[:, (m // 2) * 128:(m // 2 + 1) * 128]
        pieces.append(jnp.where(low, pltpu.roll(tile, D_ROPE, 1) if m % 2 else tile, 0.0))
    return jnp.concatenate(pieces, axis=0)


def share_kernel(rank_ref, pos_ref, inv_ref, comp_ref, out_ref, cos_ref, sin_ref, tile):
    pos = jnp.broadcast_to(pos_ref[...].astype(f32), (ROWS, ROWS)).T
    cosine, sine = cos_sin(pos * inv_ref[...])
    sine = jnp.where((lanes_of(sine.shape) & 63) < 32, -sine, sine)
    for k in range(D_LAT // 128):
        piece = slice(k * 128, (k + 1) * 128)
        tile[:ROWS, piece] = comp_ref[piece, :].astype(f32).T.astype(bf16)
    x = comp_ref[D_LAT:, :].astype(f32)
    x = jnp.concatenate([x, x], axis=0).T
    rotated = x * cosine + pltpu.roll(x, 32, 1) * sine
    for j in range(2):
        tile[ROWS:, j * 256:(j + 1) * 256] = pack_rope(rotated[j * HALF:(j + 1) * HALF]).astype(bf16)
    for i in range(N_CHIP):
        out_ref[i] = tile[...]
    cos_ref[...] = cosine
    sin_ref[...] = sine


def absorb_kernel(qn_ref, qr_ref, go_ref, uk_ref, uv_ref, cos_ref, sin_ref,
                  qt_ref, qa_ref, gt_ref, ga_ref, tall):
    contract = (((1,), (1,)), ((), ()))
    x = qr_ref[...].astype(f32)
    rotated = x * cos_ref[...] + swap_halves(x) * sin_ref[...]
    turned = pltpu.roll(rotated, HALF, 1)
    for h in range(2):
        cols = slice(h * D_NOPE, (h + 1) * D_NOPE)
        q = lax.dot_general(qn_ref[:, cols], uk_ref[:, cols], contract, preferred_element_type=f32)
        g = lax.dot_general(go_ref[:, cols], uv_ref[:, cols], contract, preferred_element_type=f32)
        rope = jnp.where(lanes_of(x.shape) < D_ROPE, rotated if h == 0 else turned, 0.0)
        for j in range(2):
            src = slice(j * HALF, (j + 1) * HALF)
            dst = slice(h * HALF, (h + 1) * HALF)
            tall[j, dst, :D_LAT] = q[src]
            tall[j, dst, D_LAT:D_PAD] = rope[src]
            tall[j, dst, D_PAD:] = g[src]
    for j in range(2):
        both = tall[j, :, :D_PAD]
        qa_ref[j] = (both * SCALE).astype(bf16)
        ga_ref[j] = tall[j, :, D_PAD:].astype(bf16)
        for k in range(D_PAD // 128):
            piece = slice(k * 128, (k + 1) * 128)
            qt_ref[j, piece, :] = (both[:, piece] * (SCALE * LOG2E)).T.astype(bf16)
        for k in range(D_LAT // 128):
            piece = slice(k * 128, (k + 1) * 128)
            gt_ref[j, piece, :] = tall[j, :, D_PAD + k * 128:D_PAD + (k + 1) * 128].T.astype(bf16)


def step_places(bm_ref, rank):
    first, second = bm_ref[0, rank], bm_ref[1, rank]
    early = jnp.where(first < second, 0, 1)
    low, high = jnp.minimum(first, second), jnp.maximum(first, second)
    count = (low + PER_CHUNK) // PER_CHUNK
    places = [(True, early, 0, low)] + [(False, 1 - early, c, high) for c in range(5)]
    for k in range(1, 4):
        is_early = k < count
        places.append((
            is_early,
            jnp.where(is_early, early, 1 - early),
            jnp.where(is_early, k, N_CHUNK - k),
            jnp.where(is_early, low, high),
        ))
    return places


def pick(flag, first, second):
    if flag is True:
        return first
    if flag is False:
        return second
    return jnp.where(flag, first, second)


def chunk_rows(c):
    return pl.ds(c * CHUNK if isinstance(c, int) else pl.multiple_of(c * CHUNK, CHUNK), CHUNK)


def attend_kernel(bm_ref, rank_ref, mine_ref, other_ref, qt_hbm, qa_hbm, gt_hbm, ga_hbm,
                  dmine_ref, dother_ref, ds_hbm, keys_hbm,
                  qt, qa, gt, ga, probs, dprobs, tops, ds, keys, place, load_sems, key_sem, ds_sems):
    sources = ((qt_hbm, qt), (gt_hbm, gt), (qa_hbm, qa), (ga_hbm, ga))
    loads = [pltpu.make_async_copy(src, dst, load_sems.at[i]) for i, (src, dst) in enumerate(sources)]
    for load in loads:
        load.start()
    rank = rank_ref[0]
    core = rank & 1
    places = step_places(bm_ref, rank)
    for chip in range(N_CHIP):
        for k, ref in enumerate((mine_ref, other_ref)):
            row = 2 * chip + (core ^ k)
            for j in range(2):
                block = bm_ref[j, row]
                place[block] = row * 2 + j
                rows = pl.ds(pl.multiple_of(block * HALF, HALF), HALF)
                keys[rows, :D_LAT] = ref[chip, j * HALF:(j + 1) * HALF, :]
                packed = ref[chip, ROWS:, j * 256:(j + 1) * 256].astype(f32)
                keys[rows, D_LAT:] = unpack_rope(packed).astype(bf16)

    moves = [pltpu.make_async_copy(keys, keys_hbm, key_sem)]
    moves[0].start()
    loads[0].wait()
    loads[1].wait()

    zero = jnp.zeros((1, LANES), f32)
    start = (jnp.full((1, LANES), HIDDEN, f32), zero, zero)
    state = {True: start, False: start}
    offset = lax.broadcasted_iota(jnp.int32, (CHUNK, LANES), 0) - (
        lax.broadcasted_iota(jnp.int32, (CHUNK, LANES), 1) & (HALF - 1)
    )
    for i, (is_early, j, c, block) in enumerate(places):
        rows = chunk_rows(c)
        top, total, weighted = (pick(is_early, a, b) for a, b in zip(state[True], state[False]))
        scores = jnp.dot(keys[rows, :], qt[j], preferred_element_type=f32)
        dp = jnp.dot(keys[rows, :D_LAT], gt[j], preferred_element_type=f32)
        scores = jnp.where(offset <= block * HALF - c * CHUNK, scores, HIDDEN)
        new_top = jnp.maximum(top, jnp.max(scores, axis=0, keepdims=True))
        e = jnp.exp2(scores - new_top)
        keep = jnp.exp2(top - new_top)
        probs[i] = e
        dprobs[i] = dp
        tops[i] = new_top
        new = (
            new_top,
            total * keep + jnp.sum(e, axis=0, keepdims=True),
            weighted * keep + jnp.sum(e * dp, axis=0, keepdims=True),
        )
        if is_early is not False:
            state[True] = tuple(pick(is_early, a, b) for a, b in zip(new, state[True]))
        if is_early is not True:
            state[False] = tuple(pick(is_early, b, a) for a, b in zip(new, state[False]))

    stats = {}
    for flag, (top, total, weighted) in state.items():
        inverse = 1.0 / total
        stats[flag] = (top, inverse, weighted * inverse)

    loads[2].wait()
    loads[3].wait()

    def change(i):
        is_early, j, c, block = places[i]
        top, inverse, delta = (pick(is_early, a, b) for a, b in zip(stats[True], stats[False]))
        p = probs[i] * (jnp.exp2(tops[i] - top) * inverse)
        d = (p * (dprobs[i] - delta)).astype(bf16)
        ds[i] = d
        moves.append(pltpu.make_async_copy(ds.at[i], ds_hbm.at[i], ds_sems.at[i]))
        moves[-1].start()
        values = jnp.dot(p.astype(bf16), ga[j], preferred_element_type=f32)
        latent = jnp.dot(d, qa[j, :, :D_LAT], preferred_element_type=f32) + values
        return latent, jnp.dot(d, qa[j, :, D_LAT:], preferred_element_type=f32)

    def put(c, parts):
        for i in range(PER_CHUNK):
            at = place[c * PER_CHUNK + i]
            chip = at // 4
            j = at & 1
            ours = ((at // 2) & 1) == core
            src = slice(i * HALF, (i + 1) * HALF)
            latent = parts[0][src].astype(bf16)
            rope = pack_rope(parts[1][src]).astype(bf16)
            rows = pl.ds(pl.multiple_of(j * HALF, HALF), HALF)
            cols = pl.ds(pl.multiple_of(j * 256, 256), 256)
            for ref, to in ((dmine_ref, jnp.where(ours, chip, N_CHIP)), (dother_ref, jnp.where(ours, N_CHIP, chip))):
                ref[to, rows, :] = latent
                ref[to, ROWS:, cols] = rope

    put(0, [a + b for a, b in zip(change(0), change(1))])
    put(4, change(5))
    for k in range(1, 4):
        is_early = places[5 + k][0]
        turn = change(5 + k)
        put(k, [a + jnp.where(is_early, b, 0.0) for a, b in zip(change(1 + k), turn)])
        put(N_CHUNK - k, [jnp.where(is_early, 0.0, b) for b in turn])
    for move in moves:
        move.wait()


def queries_kernel(bm_ref, rank_ref, keys_hbm, ds_hbm, uk_hbm, cos_ref, sin_ref, gqn_ref, gqr_ref,
                   keys, ds, uk_ref, total, sems, ds_sems):
    first = pltpu.make_async_copy(keys_hbm, keys, sems.at[0])
    weights = pltpu.make_async_copy(uk_hbm, uk_ref, sems.at[1])
    moves = [pltpu.make_async_copy(ds_hbm.at[i], ds.at[i], ds_sems.at[i]) for i in range(STEPS)]
    first.start()
    for move in moves:
        move.start()
    weights.start()
    total[...] = jnp.zeros_like(total)
    first.wait()
    for i, (_, j, c, _) in enumerate(step_places(bm_ref, rank_ref[0])):
        moves[i].wait()
        total[j] += lax.dot_general(
            ds[i], keys[chunk_rows(c), :], (((0,), (0,)), ((), ())), preferred_element_type=f32
        )
    weights.wait()
    for pair in range(HEADS // 2):
        ropes = []
        for h in (2 * pair, 2 * pair + 1):
            rows = slice(h * HALF, (h + 1) * HALF)
            both = jnp.concatenate([total[0, rows, :], total[1, rows, :]], axis=0) * SCALE
            cols = slice(h * D_NOPE, (h + 1) * D_NOPE)
            gqn_ref[:, cols] = jnp.dot(
                both[:, :D_LAT].astype(bf16), uk_ref[:, cols], preferred_element_type=f32
            ).astype(bf16)
            ropes.append(both[:, D_LAT:])
        g = jnp.where(lanes_of(ropes[0].shape) < D_ROPE, ropes[0], pltpu.roll(ropes[1], D_ROPE, 1))
        g = g * cos_ref[...] - swap_halves(g) * sin_ref[...]
        gqr_ref[:, pair * 128:(pair + 1) * 128] = g.astype(bf16)


def after_kernel(first_ref, second_ref, out_ref):
    pass


def chips_kernel(parts_ref, cos_ref, sin_ref, later_ref, out_ref):
    total = parts_ref[0].astype(f32)
    for i in range(1, N_CHIP):
        total = total + parts_ref[i].astype(f32)
    out_ref[:, :D_LAT] = total[:ROWS].astype(bf16)
    g = jnp.concatenate([unpack_rope(total[ROWS:, j * 256:(j + 1) * 256]) for j in range(2)], axis=0)
    g = g * cos_ref[...] - swap_halves(g) * sin_ref[...]
    out_ref[:, D_LAT:] = g[:, :D_ROPE].astype(bf16)


def heads_kernel(parts_ref, out_ref):
    total = parts_ref[0].astype(f32)
    for i in range(1, N_HEAD):
        total = total + parts_ref[i].astype(f32)
    total = total.astype(bf16)
    for i in range(N_HEAD):
        out_ref[i] = total


def whole(count):
    return [pl.BlockSpec(memory_space=pltpu.VMEM)] * count


def in_hbm(x):
    return pltpu.with_memory_space_constraint(x, pltpu.HBM)


def params(mib):
    return pltpu.CompilerParams(vmem_limit_bytes=mib * 1024 * 1024)


ANY = pl.BlockSpec(memory_space=pl.ANY)
HBM = pl.BlockSpec(memory_space=pltpu.HBM)
ALL_MIB = 60

SMEM = pl.BlockSpec(memory_space=pltpu.SMEM)


def attend_call(*operands):
    shape = jax.ShapeDtypeStruct
    dma = pltpu.SemaphoreType.DMA
    piece = shape((N_CHIP + 1, PACKED, D_LAT), bf16)
    return pl.pallas_call(
        attend_kernel,
        in_specs=[SMEM, SMEM] + whole(2) + [HBM] * 4,
        out_specs=(*whole(2), HBM, HBM),
        out_shape=(piece, piece, pltpu.HBM((STEPS, CHUNK, LANES), bf16), pltpu.HBM((TOTAL, D_PAD), bf16)),
        scratch_shapes=[
            pltpu.VMEM((2, D_PAD, LANES), bf16),
            pltpu.VMEM((2, LANES, D_PAD), bf16),
            pltpu.VMEM((2, D_LAT, LANES), bf16),
            pltpu.VMEM((2, LANES, D_LAT), bf16),
            pltpu.VMEM((STEPS, CHUNK, LANES), f32),
            pltpu.VMEM((STEPS, CHUNK, LANES), f32),
            pltpu.VMEM((STEPS, 1, LANES), f32),
            pltpu.VMEM((STEPS, CHUNK, LANES), bf16),
            pltpu.VMEM((TOTAL, D_PAD), bf16),
            pltpu.SMEM((N_BLOCK,), jnp.int32),
            dma((4,)),
            dma,
            dma((STEPS,)),
        ],
        compiler_params=params(36),
        name="attend",
    )(*operands)


def on_device(q_nope, q_rope, compressed, w_uk, w_uv, grad_out, positions, block_map):
    rank = lax.axis_index("ctx").astype(jnp.int32).reshape(1)
    blocks = block_map.T
    shape = jax.ShapeDtypeStruct
    table = shape((ROWS, 128), f32)
    shared, cosine, sine = pl.pallas_call(
        share_kernel,
        in_specs=[SMEM] + whole(3),
        out_specs=tuple(whole(3)),
        out_shape=(shape((N_CHIP, PACKED, D_LAT), bf16), table, table),
        scratch_shapes=[pltpu.VMEM((PACKED, D_LAT), bf16)],
        compiler_params=params(ALL_MIB),
        name="share",
    )(rank, positions.reshape(1, ROWS), jnp.asarray(frequencies()), compressed.T)
    mine = lax.all_to_all(shared, ("ctx", "head"), 0, 0, axis_index_groups=GROUPS)
    pair_cols = lambda width: pl.BlockSpec((ROWS, width), lambda p: (0, p))
    fixed = pl.BlockSpec((ROWS, 128), lambda p: (0, 0))
    weight = pl.BlockSpec((D_LAT, 256), lambda p: (0, p))
    wide = lambda rows: pl.BlockSpec((2, rows, 128), lambda p: (0, 0, p))
    tall = lambda cols: pl.BlockSpec((2, 128, cols), lambda p: (0, p, 0))
    qt, qa, gt, ga = pl.pallas_call(
        absorb_kernel,
        grid=(HEADS // 2,),
        in_specs=[pair_cols(256), pair_cols(128), pair_cols(256), weight, weight, fixed, fixed],
        out_specs=(wide(D_PAD), tall(D_PAD), wide(D_LAT), tall(D_LAT)),
        out_shape=(
            shape((2, D_PAD, LANES), bf16),
            shape((2, LANES, D_PAD), bf16),
            shape((2, D_LAT, LANES), bf16),
            shape((2, LANES, D_LAT), bf16),
        ),
        scratch_shapes=[pltpu.VMEM((2, 128, D_LAT + D_PAD), f32)],
        compiler_params=params(ALL_MIB),
        cost_estimate=pl.CostEstimate(flops=300_000_000, bytes_accessed=8_000_000, transcendentals=0),
        name="absorb",
    )(q_nope, q_rope, grad_out, w_uk, w_uv, cosine, sine)

    mine = pl.pallas_call(
        after_kernel,
        in_specs=[ANY, ANY],
        out_specs=ANY,
        out_shape=shape(mine.shape, bf16),
        input_output_aliases={0: 0},
        compiler_params=params(8),
        name="after",
    )(mine, in_hbm(qt))
    other = lax.ppermute(mine, "ctx", SWAP)
    dmine, dother, ds, keys = attend_call(blocks, rank, mine, other, *map(in_hbm, (qt, qa, gt, ga)))

    theirs = lax.ppermute(dother, "ctx", SWAP)
    summed = (dmine[:N_CHIP].astype(f32) + theirs[:N_CHIP].astype(f32)).astype(bf16)
    parts = lax.all_to_all(summed, ("ctx", "head"), 0, 0, axis_index_groups=GROUPS)

    grad_q_nope, grad_q_rope = pl.pallas_call(
        queries_kernel,
        in_specs=[SMEM, SMEM, HBM, HBM, HBM] + whole(2),
        out_specs=tuple(whole(2)),
        out_shape=(shape((ROWS, HEADS * D_NOPE), bf16), shape((ROWS, HEADS * D_ROPE), bf16)),
        scratch_shapes=[
            pltpu.VMEM((TOTAL, D_PAD), bf16),
            pltpu.VMEM((STEPS, CHUNK, LANES), bf16),
            pltpu.VMEM((D_LAT, HEADS * D_NOPE), bf16),
            pltpu.VMEM((2, LANES, D_PAD), f32),
            pltpu.SemaphoreType.DMA((2,)),
            pltpu.SemaphoreType.DMA((STEPS,)),
        ],
        compiler_params=params(ALL_MIB),
        cost_estimate=pl.CostEstimate(flops=4_000_000_000, bytes_accessed=9_000_000, transcendentals=0),
        name="queries",
    )(blocks, rank, in_hbm(keys), in_hbm(ds), in_hbm(w_uk), cosine, sine)

    owned = pl.pallas_call(
        chips_kernel,
        in_specs=whole(3) + [HBM],
        out_specs=whole(1)[0],
        out_shape=shape((ROWS, D_ALL), bf16),
        compiler_params=params(16),
        name="chips",
    )(parts, cosine, sine, in_hbm(grad_q_rope))
    slabs = lax.all_to_all(owned.reshape(N_HEAD, ROWS // N_HEAD, D_ALL), "head", 0, 0)
    slabs = pl.pallas_call(
        heads_kernel,
        in_specs=whole(1),
        out_specs=whole(1)[0],
        out_shape=shape((N_HEAD, ROWS // N_HEAD, D_ALL), bf16),
        compiler_params=params(16),
        name="heads",
    )(slabs)
    grad_compressed = lax.all_to_all(slabs, "head", 0, 0).reshape(ROWS, D_ALL)
    return grad_q_nope, grad_q_rope, grad_compressed


def solution(mesh):
    in_specs = (
        P("ctx", "head"),
        P("ctx", "head"),
        P("ctx", None),
        P(None, "head"),
        P(None, "head"),
        P("ctx", "head"),
        P("ctx"),
        P(),
    )
    out_specs = (P("ctx", "head"), P("ctx", "head"), P("ctx", None))
    return jax.shard_map(
        on_device, mesh=mesh, in_specs=in_specs, out_specs=out_specs, check_vma=False
    )
```

```python
import math

import jax
import jax.numpy as jnp
import numpy as np
from jax import lax
from jax.experimental import pallas as pl
from jax.experimental.pallas import tpu as pltpu
from jax.sharding import PartitionSpec as P

D_NOPE = 128
D_ROPE = 64
D_V = 128
D_LAT = 512
D_ALL = D_LAT + D_ROPE
D_PAD = D_LAT + 128
PACKED = 144
N_CTX = 16
N_CHIP = 8
N_HEAD = 16
ROWS = 128
HALF = 64
TOTAL = ROWS * N_CTX
HEADS = 8
LANES = HEADS * HALF
CHUNK = 256
N_CHUNK = TOTAL // CHUNK
PER_CHUNK = CHUNK // HALF
N_BLOCK = TOTAL // HALF
STEPS = N_CHUNK + 1

SCALE = (D_NOPE + D_ROPE) ** (-0.5) * (0.1 * math.log(40.0) + 1.0) ** 2
LOG2E = math.log2(math.e)
HIDDEN = -1e30

GROUPS = [
    [c * N_HEAD + ((c // 8) ^ side) * 8 + z for c in range(core, N_CTX, 2)]
    for core in range(2)
    for side in range(2)
    for z in range(8)
]
SWAP = [(c, c ^ 1) for c in range(N_CTX)]

AGAINST = (((1,), (1,)), ((), ()))

bf16 = jnp.bfloat16
f32 = jnp.float32


def frequencies():
    half = D_ROPE // 2
    index = np.arange(half, dtype=np.float64)
    width = 2 * half
    extra = np.power(10000.0, -2.0 * index / width)
    inter = extra / 40.0
    lower = math.floor(width * math.log(4096.0 / (32.0 * 2.0 * math.pi)) / (2.0 * math.log(10000.0)))
    upper = math.ceil(width * math.log(4096.0 / (1.0 * 2.0 * math.pi)) / (2.0 * math.log(10000.0)))
    lower = max(lower, 0)
    upper = min(upper, half - 1)
    spread = max(upper - lower, 0.001)
    ramp = np.clip((index - lower) / spread, 0.0, 1.0)
    inv = inter * ramp + extra * (1.0 - ramp)
    return np.tile(inv, 4).astype(np.float32)[None, :]


def split_half_pi():
    rest = math.pi / 2
    parts = []
    for bits in (9, 19):
        part = math.floor(rest * 2.0**bits) / 2.0**bits
        parts.append(part)
        rest -= part
    return parts + [rest]


HALF_PI = split_half_pi()


def cos_sin(angle):
    turns = jnp.floor(angle * (2.0 / math.pi) + 0.5)
    r = angle - turns * HALF_PI[0]
    r = r - turns * HALF_PI[1]
    r = r - turns * HALF_PI[2]
    r2 = r * r
    sine = r + r * r2 * (-1.0 / 6 + r2 * (1.0 / 120 + r2 * (-1.0 / 5040 + r2 * (1.0 / 362880))))
    cosine = 1.0 + r2 * (-0.5 + r2 * (1.0 / 24 + r2 * (-1.0 / 720 + r2 * (1.0 / 40320))))
    quarter = turns.astype(jnp.int32) & 3
    odd = (quarter & 1) == 1
    cos_out = jnp.where(odd, sine, cosine)
    sin_out = jnp.where(odd, cosine, sine)
    cos_out = jnp.where((quarter == 1) | (quarter == 2), -cos_out, cos_out)
    sin_out = jnp.where(quarter >= 2, -sin_out, sin_out)
    return cos_out, sin_out


def lanes_of(shape):
    return lax.broadcasted_iota(jnp.int32, shape, 1)


def swap_halves(x):
    return jnp.where((lanes_of(x.shape) & 63) < 32, pltpu.roll(x, 96, 1), pltpu.roll(x, 32, 1))


def pair_tile(first, second, half):
    low = lanes_of(first.shape) < HALF
    if half == 0:
        return jnp.where(low, first, pltpu.roll(second, HALF, 1))
    return jnp.where(low, pltpu.roll(first, HALF, 1), second)


def pack_rope(rope):
    low = lanes_of((16, 128)) < D_ROPE
    tiles = []
    for m in (0, 2):
        tiles.append(jnp.where(low, rope[16 * m:16 * m + 16], pltpu.roll(rope[16 * m + 16:16 * m + 32], D_ROPE, 1)))
    return jnp.concatenate(tiles, axis=1)


def unpack_rope(packed):
    low = lanes_of((16, 128)) < D_ROPE
    pieces = []
    for m in range(4):
        tile = packed[:, (m // 2) * 128:(m // 2 + 1) * 128]
        pieces.append(jnp.where(low, pltpu.roll(tile, D_ROPE, 1) if m % 2 else tile, 0.0))
    return jnp.concatenate(pieces, axis=0)


def share_kernel(rank_ref, pos_ref, inv_ref, comp_ref, out_ref, cos_ref, sin_ref, tile):
    pos = jnp.broadcast_to(pos_ref[...].astype(f32), (ROWS, ROWS)).T
    cosine, sine = cos_sin(pos * inv_ref[...])
    sine = jnp.where((lanes_of(sine.shape) & 63) < 32, -sine, sine)
    for k in range(D_LAT // 128):
        piece = slice(k * 128, (k + 1) * 128)
        tile[:ROWS, piece] = comp_ref[piece, :].astype(f32).T.astype(bf16)
    x = comp_ref[D_LAT:, :].astype(f32)
    x = jnp.concatenate([x, x], axis=0).T
    rotated = x * cosine + pltpu.roll(x, 32, 1) * sine
    for j in range(2):
        tile[ROWS:, j * 256:(j + 1) * 256] = pack_rope(rotated[j * HALF:(j + 1) * HALF]).astype(bf16)
    for i in range(N_CHIP):
        out_ref[i] = tile[...]
    cos_ref[...] = cosine
    sin_ref[...] = sine


def absorb_kernel(qn_ref, qr_ref, go_ref, uk_ref, uv_ref, cos_ref, sin_ref,
                  both_ref):
    x = qr_ref[...].astype(f32)
    rotated = x * cos_ref[...] + swap_halves(x) * sin_ref[...]
    turned = pltpu.roll(rotated, HALF, 1)
    for h in range(2):
        cols = slice(h * D_NOPE, (h + 1) * D_NOPE)
        q = lax.dot_general(qn_ref[:, cols], uk_ref[:, cols], AGAINST, preferred_element_type=f32)
        g = lax.dot_general(go_ref[:, cols], uv_ref[:, cols], AGAINST, preferred_element_type=f32)
        rope = jnp.where(lanes_of(x.shape) < D_ROPE, rotated if h == 0 else turned, 0.0)
        dst = slice(h * HALF, (h + 1) * HALF)
        for j in range(2):
            src = slice(j * HALF, (j + 1) * HALF)
            both_ref[j, 0, dst, :D_LAT] = (q[src] * SCALE).astype(bf16)
            both_ref[j, 0, dst, D_LAT:] = (rope[src] * SCALE).astype(bf16)
            both_ref[j, 1, dst, :D_LAT] = g[src].astype(bf16)
            both_ref[j, 1, dst, D_LAT:] = jnp.zeros((HALF, 128), bf16)


def step_places(bm_ref, rank):
    first, second = bm_ref[0, rank], bm_ref[1, rank]
    early = jnp.where(first < second, 0, 1)
    low, high = jnp.minimum(first, second), jnp.maximum(first, second)
    count = (low + PER_CHUNK) // PER_CHUNK
    places = [(True, early, 0, 1, low)]
    places += [(False, 1 - early, 0, 2, high), (False, 1 - early, 2, 2, high), (False, 1 - early, 4, 1, high)]
    for k in range(1, 4):
        is_early = k < count
        places.append((
            is_early,
            jnp.where(is_early, early, 1 - early),
            jnp.where(is_early, k, N_CHUNK - k),
            1,
            jnp.where(is_early, low, high),
        ))
    starts = [0, 1, 3, 5, 6, 7, 8]
    return [(slice(at * CHUNK, (at + place[3]) * CHUNK), *place) for at, place in zip(starts, places)]


def pick(flag, first, second):
    if flag is True:
        return first
    if flag is False:
        return second
    return jnp.where(flag, first, second)


def chunk_rows(c, n):
    return pl.ds(c * CHUNK if isinstance(c, int) else pl.multiple_of(c * CHUNK, CHUNK), n * CHUNK)


def attend_kernel(bm_ref, rank_ref, mine_ref, other_ref, both,
                  dmine_ref, dother_ref, ds_hbm, keys_hbm,
                  probs, dprobs, tops, ds, keys, dlat, drope, key_sem, ds_sems):
    rank = rank_ref[0]
    core = rank & 1
    places = step_places(bm_ref, rank)
    for chip in range(N_CHIP):
        for k, ref in enumerate((mine_ref, other_ref)):
            row = 2 * chip + (core ^ k)
            for j in range(2):
                block = bm_ref[j, row]
                rows = pl.ds(pl.multiple_of(block * HALF, HALF), HALF)
                keys[rows, :D_LAT] = ref[chip, j * HALF:(j + 1) * HALF, :]
                packed = ref[chip, ROWS:, j * 256:(j + 1) * 256].astype(f32)
                keys[rows, D_LAT:] = unpack_rope(packed).astype(bf16)

    moves = [pltpu.make_async_copy(keys, keys_hbm, key_sem)]
    moves[0].start()

    zero = jnp.zeros((1, LANES), f32)
    start = (jnp.full((1, LANES), HIDDEN, f32), zero, zero)
    state = {True: start, False: start}
    offset = lax.broadcasted_iota(jnp.int32, (2 * CHUNK, LANES), 0) - (
        lax.broadcasted_iota(jnp.int32, (2 * CHUNK, LANES), 1) & (HALF - 1)
    )
    for i, (at, is_early, j, c, n, block) in enumerate(places):
        rows = chunk_rows(c, n)
        top, total, weighted = (pick(is_early, a, b) for a, b in zip(state[True], state[False]))
        scores = lax.dot_general(keys[rows, :], both[j, :LANES, :], AGAINST, preferred_element_type=f32)
        dp = lax.dot_general(keys[rows, :D_LAT], both[j, LANES:, :D_LAT], AGAINST, preferred_element_type=f32)
        scores = jnp.where(offset[:n * CHUNK] <= block * HALF - c * CHUNK, scores * LOG2E, HIDDEN)
        new_top = jnp.maximum(top, jnp.max(scores, axis=0, keepdims=True))
        e = jnp.exp2(scores - new_top)
        keep = jnp.exp2(top - new_top)
        probs[at] = e
        dprobs[at] = dp
        tops[i] = new_top
        new = (
            new_top,
            total * keep + jnp.sum(e, axis=0, keepdims=True),
            weighted * keep + jnp.sum(e * dp, axis=0, keepdims=True),
        )
        if is_early is not False:
            state[True] = tuple(pick(is_early, a, b) for a, b in zip(new, state[True]))
        if is_early is not True:
            state[False] = tuple(pick(is_early, b, a) for a, b in zip(new, state[False]))

    stats = {}
    for flag, (top, total, weighted) in state.items():
        inverse = 1.0 / total
        stats[flag] = (top, inverse, weighted * inverse)

    def change(i):
        at, is_early, j, c, n, block = places[i]
        top, inverse, delta = (pick(is_early, a, b) for a, b in zip(stats[True], stats[False]))
        p = probs[at] * (jnp.exp2(tops[i] - top) * inverse)
        d = (p * (dprobs[at] - delta)).astype(bf16)
        ds[at] = d
        moves.append(pltpu.make_async_copy(ds.at[at], ds_hbm.at[at], ds_sems.at[i]))
        moves[-1].start()
        pair = jnp.concatenate([d, p.astype(bf16)], axis=1)
        latent = jnp.dot(pair, both[j, :, :D_LAT], preferred_element_type=f32)
        rope = jnp.dot(d, both[j, :LANES, D_LAT:], preferred_element_type=f32)
        return [(latent[k * CHUNK:(k + 1) * CHUNK], rope[k * CHUNK:(k + 1) * CHUNK]) for k in range(n)]

    def put(c, parts):
        rows = slice(c * CHUNK, (c + 1) * CHUNK)
        dlat[rows, :D_LAT] = parts[0].astype(bf16)
        for i in range(PER_CHUNK):
            part = parts[1][i * HALF:(i + 1) * HALF]
            drope[(c * PER_CHUNK + i) * 16:(c * PER_CHUNK + i + 1) * 16, :] = pack_rope(part).astype(bf16)

    early = change(0)
    for k in range(1, 4):
        turn = change(3 + k)[0]
        is_early = places[3 + k][1]
        put(N_CHUNK - k, [jnp.where(is_early, 0.0, x) for x in turn])
        early.append([jnp.where(is_early, x, 0.0) for x in turn])
    late = change(1) + change(2) + change(3)
    for c in range(4):
        put(c, [x + y for x, y in zip(late[c], early[c])])
    put(4, late[4])
    for chip in range(N_CHIP):
        for k, ref in enumerate((dmine_ref, dother_ref)):
            row = 2 * chip + (core ^ k)
            for j in range(2):
                block = bm_ref[j, row]
                ref[chip, j * HALF:(j + 1) * HALF, :] = dlat[pl.ds(pl.multiple_of(block * HALF, HALF), HALF), :]
                ref[chip, ROWS:, j * 256:(j + 1) * 256] = drope[pl.ds(pl.multiple_of(block * 16, 16), 16), :]
    for move in moves:
        move.wait()


def queries_kernel(bm_ref, rank_ref, keys_hbm, ds_hbm, uk_hbm, cos_ref, sin_ref, gqn_ref, gqr_ref,
                   keys, ds, uk_ref, total, sems, ds_sems):
    first = pltpu.make_async_copy(keys_hbm, keys, sems.at[0])
    weights = pltpu.make_async_copy(uk_hbm, uk_ref, sems.at[1])
    places = step_places(bm_ref, rank_ref[0])
    moves = [pltpu.make_async_copy(ds_hbm.at[p[0]], ds.at[p[0]], ds_sems.at[i]) for i, p in enumerate(places)]
    first.start()
    for move in moves:
        move.start()
    weights.start()
    total[...] = jnp.zeros_like(total)
    first.wait()
    for move, (at, _, j, c, n, _) in zip(moves, places):
        move.wait()
        total[j] += lax.dot_general(
            ds[at], keys[chunk_rows(c, n), :], (((0,), (0,)), ((), ())), preferred_element_type=f32
        )
    weights.wait()
    for pair in range(HEADS // 2):
        ropes = []
        for h in (2 * pair, 2 * pair + 1):
            rows = slice(h * HALF, (h + 1) * HALF)
            both = jnp.concatenate([total[0, rows, :], total[1, rows, :]], axis=0) * SCALE
            cols = slice(h * D_NOPE, (h + 1) * D_NOPE)
            gqn_ref[:, cols] = jnp.dot(
                both[:, :D_LAT].astype(bf16), uk_ref[:, cols], preferred_element_type=f32
            ).astype(bf16)
            ropes.append(both[:, D_LAT:])
        g = jnp.where(lanes_of(ropes[0].shape) < D_ROPE, ropes[0], pltpu.roll(ropes[1], D_ROPE, 1))
        g = g * cos_ref[...] - swap_halves(g) * sin_ref[...]
        gqr_ref[:, pair * 128:(pair + 1) * 128] = g.astype(bf16)


def after_kernel(first_ref, second_ref, out_ref):
    pass


def chips_kernel(parts_ref, cos_ref, sin_ref, later_ref, out_ref):
    total = parts_ref[0].astype(f32)
    for i in range(1, N_CHIP):
        total = total + parts_ref[i].astype(f32)
    out_ref[:, :D_LAT] = total[:ROWS].astype(bf16)
    g = jnp.concatenate([unpack_rope(total[ROWS:, j * 256:(j + 1) * 256]) for j in range(2)], axis=0)
    g = g * cos_ref[...] - swap_halves(g) * sin_ref[...]
    out_ref[:, D_LAT:] = g[:, :D_ROPE].astype(bf16)


def heads_kernel(parts_ref, out_ref):
    total = parts_ref[0].astype(f32)
    for i in range(1, N_HEAD):
        total = total + parts_ref[i].astype(f32)
    total = total.astype(bf16)
    for i in range(N_HEAD):
        out_ref[i] = total


def whole(count):
    return [pl.BlockSpec(memory_space=pltpu.VMEM)] * count


def in_hbm(x):
    return pltpu.with_memory_space_constraint(x, pltpu.HBM)


def params(mib):
    return pltpu.CompilerParams(vmem_limit_bytes=mib * 1024 * 1024)


ANY = pl.BlockSpec(memory_space=pl.ANY)
HBM = pl.BlockSpec(memory_space=pltpu.HBM)
ALL_MIB = 60

SMEM = pl.BlockSpec(memory_space=pltpu.SMEM)


def attend_call(*operands):
    shape = jax.ShapeDtypeStruct
    dma = pltpu.SemaphoreType.DMA
    piece = shape((N_CHIP, PACKED, D_LAT), bf16)
    return pl.pallas_call(
        attend_kernel,
        in_specs=[SMEM, SMEM] + whole(3),
        out_specs=(*whole(2), HBM, HBM),
        out_shape=(piece, piece, pltpu.HBM((STEPS * CHUNK, LANES), bf16), pltpu.HBM((TOTAL, D_PAD), bf16)),
        scratch_shapes=[
            pltpu.VMEM((STEPS * CHUNK, LANES), f32),
            pltpu.VMEM((STEPS * CHUNK, LANES), f32),
            pltpu.VMEM((STEPS, 1, LANES), f32),
            pltpu.VMEM((STEPS * CHUNK, LANES), bf16),
            pltpu.VMEM((TOTAL, D_PAD), bf16),
            pltpu.VMEM((TOTAL, D_LAT), bf16),
            pltpu.VMEM((N_BLOCK * 16, 256), bf16),
            dma,
            dma((STEPS,)),
        ],
        compiler_params=params(36),
        name="attend",
    )(*operands)


def on_device(q_nope, q_rope, compressed, w_uk, w_uv, grad_out, positions, block_map):
    rank = lax.axis_index("ctx").astype(jnp.int32).reshape(1)
    blocks = block_map.T
    shape = jax.ShapeDtypeStruct
    table = shape((ROWS, 128), f32)
    shared, cosine, sine = pl.pallas_call(
        share_kernel,
        in_specs=[SMEM] + whole(3),
        out_specs=tuple(whole(3)),
        out_shape=(shape((N_CHIP, PACKED, D_LAT), bf16), table, table),
        scratch_shapes=[pltpu.VMEM((PACKED, D_LAT), bf16)],
        compiler_params=params(ALL_MIB),
        name="share",
    )(rank, positions.reshape(1, ROWS), jnp.asarray(frequencies()), compressed.T)
    mine = lax.all_to_all(shared, ("ctx", "head"), 0, 0, axis_index_groups=GROUPS)
    pair_cols = lambda width: pl.BlockSpec((ROWS, width), lambda p: (0, p))
    fixed = pl.BlockSpec((ROWS, 128), lambda p: (0, 0))
    weight = pl.BlockSpec((D_LAT, 256), lambda p: (0, p))
    both = pl.pallas_call(
        absorb_kernel,
        grid=(HEADS // 2,),
        in_specs=[pair_cols(256), pair_cols(128), pair_cols(256), weight, weight, fixed, fixed],
        out_specs=pl.BlockSpec((2, 2, 128, D_PAD), lambda p: (0, 0, p, 0)),
        out_shape=shape((2, 2, LANES, D_PAD), bf16),
        compiler_params=params(ALL_MIB),
        cost_estimate=pl.CostEstimate(flops=300_000_000, bytes_accessed=8_000_000, transcendentals=0),
        name="absorb",
    )(q_nope, q_rope, grad_out, w_uk, w_uv, cosine, sine)

    mine = pl.pallas_call(
        after_kernel,
        in_specs=[ANY, ANY],
        out_specs=ANY,
        out_shape=shape(mine.shape, bf16),
        input_output_aliases={0: 0},
        compiler_params=params(8),
        name="after",
    )(mine, in_hbm(both))
    both = both.reshape(2, 2 * LANES, D_PAD)
    other = lax.ppermute(mine, "ctx", SWAP)
    dmine, dother, ds, keys = attend_call(blocks, rank, mine, other, both)

    theirs = lax.ppermute(dother, "ctx", SWAP)
    summed = (dmine.astype(f32) + theirs.astype(f32)).astype(bf16)
    parts = lax.all_to_all(summed, ("ctx", "head"), 0, 0, axis_index_groups=GROUPS)

    grad_q_nope, grad_q_rope = pl.pallas_call(
        queries_kernel,
        in_specs=[SMEM, SMEM, HBM, HBM, HBM] + whole(2),
        out_specs=tuple(whole(2)),
        out_shape=(shape((ROWS, HEADS * D_NOPE), bf16), shape((ROWS, HEADS * D_ROPE), bf16)),
        scratch_shapes=[
            pltpu.VMEM((TOTAL, D_PAD), bf16),
            pltpu.VMEM((STEPS * CHUNK, LANES), bf16),
            pltpu.VMEM((D_LAT, HEADS * D_NOPE), bf16),
            pltpu.VMEM((2, LANES, D_PAD), f32),
            pltpu.SemaphoreType.DMA((2,)),
            pltpu.SemaphoreType.DMA((STEPS,)),
        ],
        compiler_params=params(ALL_MIB),
        cost_estimate=pl.CostEstimate(flops=4_000_000_000, bytes_accessed=9_000_000, transcendentals=0),
        name="queries",
    )(blocks, rank, in_hbm(keys), in_hbm(ds), in_hbm(w_uk), cosine, sine)

    owned = pl.pallas_call(
        chips_kernel,
        in_specs=whole(3) + [HBM],
        out_specs=whole(1)[0],
        out_shape=shape((ROWS, D_ALL), bf16),
        compiler_params=params(16),
        name="chips",
    )(parts, cosine, sine, in_hbm(grad_q_rope))
    slabs = lax.all_to_all(owned.reshape(N_HEAD, ROWS // N_HEAD, D_ALL), "head", 0, 0)
    slabs = pl.pallas_call(
        heads_kernel,
        in_specs=whole(1),
        out_specs=whole(1)[0],
        out_shape=shape((N_HEAD, ROWS // N_HEAD, D_ALL), bf16),
        compiler_params=params(16),
        name="heads",
    )(slabs)
    grad_compressed = lax.all_to_all(slabs, "head", 0, 0).reshape(ROWS, D_ALL)
    return grad_q_nope, grad_q_rope, grad_compressed


def solution(mesh):
    in_specs = (
        P("ctx", "head"),
        P("ctx", "head"),
        P("ctx", None),
        P(None, "head"),
        P(None, "head"),
        P("ctx", "head"),
        P("ctx"),
        P(),
    )
    out_specs = (P("ctx", "head"), P("ctx", "head"), P("ctx", None))
    return jax.shard_map(
        on_device, mesh=mesh, in_specs=in_specs, out_specs=out_specs, check_vma=False
    )
```

```python
import math

import jax
import jax.numpy as jnp
import numpy as np
from jax import lax
from jax.experimental import pallas as pl
from jax.experimental.pallas import tpu as pltpu
from jax.sharding import PartitionSpec as P

D_NOPE = 128
D_ROPE = 64
D_V = 128
D_LAT = 512
D_ALL = D_LAT + D_ROPE
D_PAD = D_LAT + 128
PACKED = 144
N_CTX = 16
N_CHIP = 8
N_HEAD = 16
ROWS = 128
HALF = 64
TOTAL = ROWS * N_CTX
HEADS = 8
LANES = HEADS * HALF
CHUNK = 256
N_CHUNK = TOTAL // CHUNK
PER_CHUNK = CHUNK // HALF
N_BLOCK = TOTAL // HALF
STEPS = N_CHUNK + 1

SCALE = (D_NOPE + D_ROPE) ** (-0.5) * (0.1 * math.log(40.0) + 1.0) ** 2
LOG2E = math.log2(math.e)
HIDDEN = -1e30

GROUPS = [
    [c * N_HEAD + ((c // 8) ^ side) * 8 + z for c in range(core, N_CTX, 2)]
    for core in range(2)
    for side in range(2)
    for z in range(8)
]
ALONG_X = [(i, i ^ (8 * N_HEAD + 8)) for i in range(N_CTX * N_HEAD)]
ALONG_Y1 = [(c, c ^ 2) for c in range(N_CTX)]
ALONG_Y3 = [(c, c ^ 6) for c in range(N_CTX)]
OWNERS = (0, 2, 4, 6, 8, 10, 12, 14)
SWAP = [(c, c ^ 1) for c in range(N_CTX)]

AGAINST = (((1,), (1,)), ((), ()))

bf16 = jnp.bfloat16
f32 = jnp.float32


def frequencies():
    half = D_ROPE // 2
    index = np.arange(half, dtype=np.float64)
    width = 2 * half
    extra = np.power(10000.0, -2.0 * index / width)
    inter = extra / 40.0
    lower = math.floor(width * math.log(4096.0 / (32.0 * 2.0 * math.pi)) / (2.0 * math.log(10000.0)))
    upper = math.ceil(width * math.log(4096.0 / (1.0 * 2.0 * math.pi)) / (2.0 * math.log(10000.0)))
    lower = max(lower, 0)
    upper = min(upper, half - 1)
    spread = max(upper - lower, 0.001)
    ramp = np.clip((index - lower) / spread, 0.0, 1.0)
    inv = inter * ramp + extra * (1.0 - ramp)
    return np.tile(inv, 4).astype(np.float32)[None, :]


def split_half_pi():
    rest = math.pi / 2
    parts = []
    for bits in (9, 19):
        part = math.floor(rest * 2.0**bits) / 2.0**bits
        parts.append(part)
        rest -= part
    return parts + [rest]


HALF_PI = split_half_pi()


def cos_sin(angle):
    turns = jnp.floor(angle * (2.0 / math.pi) + 0.5)
    r = angle - turns * HALF_PI[0]
    r = r - turns * HALF_PI[1]
    r = r - turns * HALF_PI[2]
    r2 = r * r
    sine = r + r * r2 * (-1.0 / 6 + r2 * (1.0 / 120 + r2 * (-1.0 / 5040 + r2 * (1.0 / 362880))))
    cosine = 1.0 + r2 * (-0.5 + r2 * (1.0 / 24 + r2 * (-1.0 / 720 + r2 * (1.0 / 40320))))
    quarter = turns.astype(jnp.int32) & 3
    odd = (quarter & 1) == 1
    cos_out = jnp.where(odd, sine, cosine)
    sin_out = jnp.where(odd, cosine, sine)
    cos_out = jnp.where((quarter == 1) | (quarter == 2), -cos_out, cos_out)
    sin_out = jnp.where(quarter >= 2, -sin_out, sin_out)
    return cos_out, sin_out


def lanes_of(shape):
    return lax.broadcasted_iota(jnp.int32, shape, 1)


def swap_halves(x):
    return jnp.where((lanes_of(x.shape) & 63) < 32, pltpu.roll(x, 96, 1), pltpu.roll(x, 32, 1))


def pair_tile(first, second, half):
    low = lanes_of(first.shape) < HALF
    if half == 0:
        return jnp.where(low, first, pltpu.roll(second, HALF, 1))
    return jnp.where(low, pltpu.roll(first, HALF, 1), second)


def pack_rope(rope):
    low = lanes_of((16, 128)) < D_ROPE
    tiles = []
    for m in (0, 2):
        tiles.append(jnp.where(low, rope[16 * m:16 * m + 16], pltpu.roll(rope[16 * m + 16:16 * m + 32], D_ROPE, 1)))
    return jnp.concatenate(tiles, axis=1)


def unpack_rope(packed):
    low = lanes_of((16, 128)) < D_ROPE
    pieces = []
    for m in range(4):
        tile = packed[:, (m // 2) * 128:(m // 2 + 1) * 128]
        pieces.append(jnp.where(low, pltpu.roll(tile, D_ROPE, 1) if m % 2 else tile, 0.0))
    return jnp.concatenate(pieces, axis=0)


def share_kernel(rank_ref, pos_ref, inv_ref, comp_ref, tile, cos_ref, sin_ref):
    pos = jnp.broadcast_to(pos_ref[...].astype(f32), (ROWS, ROWS)).T
    cosine, sine = cos_sin(pos * inv_ref[...])
    sine = jnp.where((lanes_of(sine.shape) & 63) < 32, -sine, sine)
    for k in range(D_LAT // 128):
        piece = slice(k * 128, (k + 1) * 128)
        tile[:ROWS, piece] = comp_ref[piece, :].astype(f32).T.astype(bf16)
    x = comp_ref[D_LAT:, :].astype(f32)
    x = jnp.concatenate([x, x], axis=0).T
    rotated = x * cosine + pltpu.roll(x, 32, 1) * sine
    for j in range(2):
        tile[ROWS:, j * 256:(j + 1) * 256] = pack_rope(rotated[j * HALF:(j + 1) * HALF]).astype(bf16)
    cos_ref[...] = cosine
    sin_ref[...] = sine


def absorb_kernel(qn_ref, qr_ref, go_ref, uk_ref, uv_ref, cos_ref, sin_ref,
                  both_ref):
    x = qr_ref[...].astype(f32)
    rotated = x * cos_ref[...] + swap_halves(x) * sin_ref[...]
    turned = pltpu.roll(rotated, HALF, 1)
    for h in range(2):
        cols = slice(h * D_NOPE, (h + 1) * D_NOPE)
        q = lax.dot_general(qn_ref[:, cols], uk_ref[:, cols], AGAINST, preferred_element_type=f32)
        g = lax.dot_general(go_ref[:, cols], uv_ref[:, cols], AGAINST, preferred_element_type=f32)
        rope = jnp.where(lanes_of(x.shape) < D_ROPE, rotated if h == 0 else turned, 0.0)
        dst = slice(h * HALF, (h + 1) * HALF)
        for j in range(2):
            src = slice(j * HALF, (j + 1) * HALF)
            both_ref[j, 0, dst, :D_LAT] = (q[src] * SCALE).astype(bf16)
            both_ref[j, 0, dst, D_LAT:] = (rope[src] * SCALE).astype(bf16)
            both_ref[j, 1, dst, :D_LAT] = g[src].astype(bf16)
            both_ref[j, 1, dst, D_LAT:] = jnp.zeros((HALF, 128), bf16)


def step_places(bm_ref, rank):
    first, second = bm_ref[0, rank], bm_ref[1, rank]
    early = jnp.where(first < second, 0, 1)
    low, high = jnp.minimum(first, second), jnp.maximum(first, second)
    count = (low + PER_CHUNK) // PER_CHUNK
    places = [(True, early, 0, 1, low)]
    places += [(False, 1 - early, 0, 2, high), (False, 1 - early, 2, 2, high), (False, 1 - early, 4, 1, high)]
    for k in range(1, 4):
        is_early = k < count
        places.append((
            is_early,
            jnp.where(is_early, early, 1 - early),
            jnp.where(is_early, k, N_CHUNK - k),
            1,
            jnp.where(is_early, low, high),
        ))
    starts = [0, 1, 3, 5, 6, 7, 8]
    return [(slice(at * CHUNK, (at + place[3]) * CHUNK), *place) for at, place in zip(starts, places)]


def pick(flag, first, second):
    if flag is True:
        return first
    if flag is False:
        return second
    return jnp.where(flag, first, second)


def chunk_rows(c, n):
    return pl.ds(c * CHUNK if isinstance(c, int) else pl.multiple_of(c * CHUNK, CHUNK), n * CHUNK)


def attend_kernel(bm_ref, rank_ref, both, *refs):
    shares, refs = refs[:2 * N_CHIP], refs[2 * N_CHIP:]
    dmine_ref, dother_ref, ds, keys, probs, dprobs, tops, dlat, drope = refs
    rank = rank_ref[0]
    core = rank & 1
    places = step_places(bm_ref, rank)
    for i, ref in enumerate(shares):
        row = rank ^ (OWNERS[i % N_CHIP] ^ (i // N_CHIP))
        for j in range(2):
            rows = pl.ds(pl.multiple_of(bm_ref[j, row] * HALF, HALF), HALF)
            keys[rows, :D_LAT] = ref[j * HALF:(j + 1) * HALF, :]
            packed = ref[ROWS:, j * 256:(j + 1) * 256].astype(f32)
            keys[rows, D_LAT:] = unpack_rope(packed).astype(bf16)

    zero = jnp.zeros((1, LANES), f32)
    start = (jnp.full((1, LANES), HIDDEN, f32), zero, zero)
    state = {True: start, False: start}
    offset = lax.broadcasted_iota(jnp.int32, (2 * CHUNK, LANES), 0) - (
        lax.broadcasted_iota(jnp.int32, (2 * CHUNK, LANES), 1) & (HALF - 1)
    )
    for i, (at, is_early, j, c, n, block) in enumerate(places):
        rows = chunk_rows(c, n)
        top, total, weighted = (pick(is_early, a, b) for a, b in zip(state[True], state[False]))
        scores = lax.dot_general(keys[rows, :], both[j, :LANES, :], AGAINST, preferred_element_type=f32)
        dp = lax.dot_general(keys[rows, :D_LAT], both[j, LANES:, :D_LAT], AGAINST, preferred_element_type=f32)
        scores = jnp.where(offset[:n * CHUNK] <= block * HALF - c * CHUNK, scores * LOG2E, HIDDEN)
        new_top = jnp.maximum(top, jnp.max(scores, axis=0, keepdims=True))
        e = jnp.exp2(scores - new_top)
        keep = jnp.exp2(top - new_top)
        probs[at] = e
        dprobs[at] = dp
        tops[i] = new_top
        new = (
            new_top,
            total * keep + jnp.sum(e, axis=0, keepdims=True),
            weighted * keep + jnp.sum(e * dp, axis=0, keepdims=True),
        )
        if is_early is not False:
            state[True] = tuple(pick(is_early, a, b) for a, b in zip(new, state[True]))
        if is_early is not True:
            state[False] = tuple(pick(is_early, b, a) for a, b in zip(new, state[False]))

    stats = {}
    for flag, (top, total, weighted) in state.items():
        inverse = 1.0 / total
        stats[flag] = (top, inverse, weighted * inverse)

    def change(i):
        at, is_early, j, c, n, block = places[i]
        top, inverse, delta = (pick(is_early, a, b) for a, b in zip(stats[True], stats[False]))
        p = probs[at] * (jnp.exp2(tops[i] - top) * inverse)
        d = (p * (dprobs[at] - delta)).astype(bf16)
        ds[at] = d
        pair = jnp.concatenate([d, p.astype(bf16)], axis=1)
        latent = jnp.dot(pair, both[j, :, :D_LAT], preferred_element_type=f32)
        rope = jnp.dot(d, both[j, :LANES, D_LAT:], preferred_element_type=f32)
        return [(latent[k * CHUNK:(k + 1) * CHUNK], rope[k * CHUNK:(k + 1) * CHUNK]) for k in range(n)]

    def put(c, parts):
        rows = slice(c * CHUNK, (c + 1) * CHUNK)
        dlat[rows, :D_LAT] = parts[0].astype(bf16)
        for i in range(PER_CHUNK):
            part = parts[1][i * HALF:(i + 1) * HALF]
            drope[(c * PER_CHUNK + i) * 16:(c * PER_CHUNK + i + 1) * 16, :] = pack_rope(part).astype(bf16)

    early = change(0)
    for k in range(1, 4):
        turn = change(3 + k)[0]
        is_early = places[3 + k][1]
        put(N_CHUNK - k, [jnp.where(is_early, 0.0, x) for x in turn])
        early.append([jnp.where(is_early, x, 0.0) for x in turn])
    late = change(1) + change(2) + change(3)
    for c in range(4):
        put(c, [x + y for x, y in zip(late[c], early[c])])
    put(4, late[4])
    for chip in range(N_CHIP):
        for k, ref in enumerate((dmine_ref, dother_ref)):
            row = 2 * chip + (core ^ k)
            for j in range(2):
                block = bm_ref[j, row]
                ref[chip, j * HALF:(j + 1) * HALF, :] = dlat[pl.ds(pl.multiple_of(block * HALF, HALF), HALF), :]
                ref[chip, ROWS:, j * 256:(j + 1) * 256] = drope[pl.ds(pl.multiple_of(block * 16, 16), 16), :]


def spill_kernel(ds, keys, ds_hbm, keys_hbm, sems):
    copies = [pltpu.make_async_copy(ds, ds_hbm, sems.at[0]), pltpu.make_async_copy(keys, keys_hbm, sems.at[1])]
    for copy in copies:
        copy.start()
    for copy in copies:
        copy.wait()


def queries_kernel(bm_ref, rank_ref, keys_hbm, ds_hbm, uk_hbm, cos_ref, sin_ref, gqn_ref, gqr_ref,
                   keys, ds, uk_ref, total, sems, ds_sems):
    first = pltpu.make_async_copy(keys_hbm, keys, sems.at[0])
    weights = pltpu.make_async_copy(uk_hbm, uk_ref, sems.at[1])
    places = step_places(bm_ref, rank_ref[0])
    moves = [pltpu.make_async_copy(ds_hbm.at[p[0]], ds.at[p[0]], ds_sems.at[i]) for i, p in enumerate(places)]
    first.start()
    for move in moves:
        move.start()
    weights.start()
    total[...] = jnp.zeros_like(total)
    first.wait()
    for move, (at, _, j, c, n, _) in zip(moves, places):
        move.wait()
        total[j] += lax.dot_general(
            ds[at], keys[chunk_rows(c, n), :], (((0,), (0,)), ((), ())), preferred_element_type=f32
        )
    weights.wait()
    for pair in range(HEADS // 2):
        ropes = []
        for h in (2 * pair, 2 * pair + 1):
            rows = slice(h * HALF, (h + 1) * HALF)
            both = jnp.concatenate([total[0, rows, :], total[1, rows, :]], axis=0) * SCALE
            cols = slice(h * D_NOPE, (h + 1) * D_NOPE)
            gqn_ref[:, cols] = jnp.dot(
                both[:, :D_LAT].astype(bf16), uk_ref[:, cols], preferred_element_type=f32
            ).astype(bf16)
            ropes.append(both[:, D_LAT:])
        g = jnp.where(lanes_of(ropes[0].shape) < D_ROPE, ropes[0], pltpu.roll(ropes[1], D_ROPE, 1))
        g = g * cos_ref[...] - swap_halves(g) * sin_ref[...]
        gqr_ref[:, pair * 128:(pair + 1) * 128] = g.astype(bf16)


def after_kernel(first_ref, second_ref, out_ref):
    pass


def pair_kernel(ours_ref, theirs_ref, later_ref, out_ref):
    for i in range(N_CHIP):
        out_ref[i] = (ours_ref[i].astype(f32) + theirs_ref[i].astype(f32)).astype(bf16)


def chips_kernel(parts_ref, cos_ref, sin_ref, later_ref, out_ref):
    total = parts_ref[0].astype(f32)
    for i in range(1, N_CHIP):
        total = total + parts_ref[i].astype(f32)
    out_ref[:, :D_LAT] = total[:ROWS].astype(bf16)
    g = jnp.concatenate([unpack_rope(total[ROWS:, j * 256:(j + 1) * 256]) for j in range(2)], axis=0)
    g = g * cos_ref[...] - swap_halves(g) * sin_ref[...]
    out_ref[:, D_LAT:] = g[:, :D_ROPE].astype(bf16)


def heads_kernel(parts_ref, out_ref):
    total = parts_ref[0].astype(f32)
    for i in range(1, N_HEAD):
        total = total + parts_ref[i].astype(f32)
    total = total.astype(bf16)
    for i in range(N_HEAD):
        out_ref[i] = total


def whole(count):
    return [pl.BlockSpec(memory_space=pltpu.VMEM)] * count


def in_hbm(x):
    return pltpu.with_memory_space_constraint(x, pltpu.HBM)


def params(mib):
    return pltpu.CompilerParams(vmem_limit_bytes=mib * 1024 * 1024)


ANY = pl.BlockSpec(memory_space=pl.ANY)
HBM = pl.BlockSpec(memory_space=pltpu.HBM)
ALL_MIB = 60

SMEM = pl.BlockSpec(memory_space=pltpu.SMEM)


def attend_call(*operands):
    shape = jax.ShapeDtypeStruct
    piece = shape((N_CHIP, PACKED, D_LAT), bf16)
    return pl.pallas_call(
        attend_kernel,
        in_specs=[SMEM, SMEM] + whole(1 + 2 * N_CHIP),
        out_specs=tuple(whole(4)),
        out_shape=(piece, piece, shape((STEPS * CHUNK, LANES), bf16), shape((TOTAL, D_PAD), bf16)),
        scratch_shapes=[
            pltpu.VMEM((STEPS * CHUNK, LANES), f32),
            pltpu.VMEM((STEPS * CHUNK, LANES), f32),
            pltpu.VMEM((STEPS, 1, LANES), f32),
            pltpu.VMEM((TOTAL, D_LAT), bf16),
            pltpu.VMEM((N_BLOCK * 16, 256), bf16),
        ],
        compiler_params=params(36),
        name="attend",
    )(*operands)


def on_device(q_nope, q_rope, compressed, w_uk, w_uv, grad_out, positions, block_map):
    rank = lax.axis_index("ctx").astype(jnp.int32).reshape(1)
    blocks = block_map.T
    shape = jax.ShapeDtypeStruct
    table = shape((ROWS, 128), f32)
    shared, cosine, sine = pl.pallas_call(
        share_kernel,
        in_specs=[SMEM] + whole(3),
        out_specs=tuple(whole(3)),
        out_shape=(shape((PACKED, D_LAT), bf16), table, table),
        compiler_params=params(ALL_MIB),
        name="share",
    )(rank, positions.reshape(1, ROWS), jnp.asarray(frequencies()), compressed.T)
    x = lambda a: lax.ppermute(a, ("ctx", "head"), ALONG_X)
    y1 = lambda a: lax.ppermute(a, "ctx", ALONG_Y1)
    y3 = lambda a: lax.ppermute(a, "ctx", ALONG_Y3)
    swap = lambda a: lax.ppermute(a, "ctx", SWAP)
    held = {0: shared, 8: x(shared), 2: y1(shared), 6: y3(shared)}
    held.update({10: y1(held[8]), 4: y3(held[2]), 14: x(held[6])})
    pair_cols = lambda width: pl.BlockSpec((ROWS, width), lambda p: (0, p))
    fixed = pl.BlockSpec((ROWS, 128), lambda p: (0, 0))
    weight = pl.BlockSpec((D_LAT, 256), lambda p: (0, p))
    both = pl.pallas_call(
        absorb_kernel,
        grid=(HEADS // 2,),
        in_specs=[pair_cols(256), pair_cols(128), pair_cols(256), weight, weight, fixed, fixed],
        out_specs=pl.BlockSpec((2, 2, 128, D_PAD), lambda p: (0, 0, p, 0)),
        out_shape=shape((2, 2, LANES, D_PAD), bf16),
        compiler_params=params(16),
        cost_estimate=pl.CostEstimate(flops=300_000_000, bytes_accessed=8_000_000, transcendentals=0),
        name="absorb",
    )(*map(in_hbm, (q_nope, q_rope, grad_out, w_uk, w_uv, cosine, sine)))

    held[4] = pl.pallas_call(
        after_kernel,
        in_specs=[ANY, ANY],
        out_specs=ANY,
        out_shape=shape((PACKED, D_LAT), bf16),
        input_output_aliases={0: 0},
        compiler_params=params(8),
        name="after",
    )(held[4], both)
    held[12] = x(held[4])
    mine = [held[owner] for owner in OWNERS]
    other = [swap(share) for share in mine]
    both = both.reshape(2, 2 * LANES, D_PAD)
    dmine, dother, ds, keys = attend_call(blocks, rank, both, *mine, *other)
    ds, keys = pl.pallas_call(
        spill_kernel,
        in_specs=[ANY, ANY],
        out_specs=(HBM, HBM),
        out_shape=(pltpu.HBM(ds.shape, bf16), pltpu.HBM(keys.shape, bf16)),
        scratch_shapes=[pltpu.SemaphoreType.DMA((2,))],
        compiler_params=params(8),
        cost_estimate=pl.CostEstimate(flops=0, bytes_accessed=10_000_000, transcendentals=0),
        name="spill",
    )(ds, keys)

    theirs = lax.ppermute(dother, "ctx", SWAP)
    summed = pl.pallas_call(
        pair_kernel,
        in_specs=whole(2) + [HBM],
        out_specs=whole(1)[0],
        out_shape=shape(dmine.shape, bf16),
        compiler_params=params(16),
        name="pair",
    )(dmine, theirs, in_hbm(ds))
    parts = lax.all_to_all(summed, ("ctx", "head"), 0, 0, axis_index_groups=GROUPS)

    grad_q_nope, grad_q_rope = pl.pallas_call(
        queries_kernel,
        in_specs=[SMEM, SMEM, HBM, HBM, HBM] + whole(2),
        out_specs=tuple(whole(2)),
        out_shape=(shape((ROWS, HEADS * D_NOPE), bf16), shape((ROWS, HEADS * D_ROPE), bf16)),
        scratch_shapes=[
            pltpu.VMEM((TOTAL, D_PAD), bf16),
            pltpu.VMEM((STEPS * CHUNK, LANES), bf16),
            pltpu.VMEM((D_LAT, HEADS * D_NOPE), bf16),
            pltpu.VMEM((2, LANES, D_PAD), f32),
            pltpu.SemaphoreType.DMA((2,)),
            pltpu.SemaphoreType.DMA((STEPS,)),
        ],
        compiler_params=params(ALL_MIB),
        cost_estimate=pl.CostEstimate(flops=4_000_000_000, bytes_accessed=9_000_000, transcendentals=0),
        name="queries",
    )(blocks, rank, in_hbm(keys), in_hbm(ds), in_hbm(w_uk), cosine, sine)

    owned = pl.pallas_call(
        chips_kernel,
        in_specs=whole(3) + [HBM],
        out_specs=whole(1)[0],
        out_shape=shape((ROWS, D_ALL), bf16),
        compiler_params=params(16),
        name="chips",
    )(parts, cosine, sine, in_hbm(grad_q_rope))
    slabs = lax.all_to_all(owned.reshape(N_HEAD, ROWS // N_HEAD, D_ALL), "head", 0, 0)
    slabs = pl.pallas_call(
        heads_kernel,
        in_specs=whole(1),
        out_specs=whole(1)[0],
        out_shape=shape((N_HEAD, ROWS // N_HEAD, D_ALL), bf16),
        compiler_params=params(16),
        name="heads",
    )(slabs)
    grad_compressed = lax.all_to_all(slabs, "head", 0, 0).reshape(ROWS, D_ALL)
    return grad_q_nope, grad_q_rope, grad_compressed


def solution(mesh):
    in_specs = (
        P("ctx", "head"),
        P("ctx", "head"),
        P("ctx", None),
        P(None, "head"),
        P(None, "head"),
        P("ctx", "head"),
        P("ctx"),
        P(),
    )
    out_specs = (P("ctx", "head"), P("ctx", "head"), P("ctx", None))
    return jax.shard_map(
        on_device, mesh=mesh, in_specs=in_specs, out_specs=out_specs, check_vma=False
    )
```

```python
import math

import jax
import jax.numpy as jnp
import numpy as np
from jax import lax
from jax.experimental import pallas as pl
from jax.experimental.pallas import tpu as pltpu
from jax.sharding import PartitionSpec as P

D_NOPE = 128
D_ROPE = 64
D_V = 128
D_LAT = 512
D_ALL = D_LAT + D_ROPE
D_PAD = D_LAT + 128
PACKED = 144
N_CTX = 16
N_CHIP = 8
N_HEAD = 16
ROWS = 128
HALF = 64
TOTAL = ROWS * N_CTX
HEADS = 8
LANES = HEADS * HALF
CHUNK = 256
N_CHUNK = TOTAL // CHUNK
PER_CHUNK = CHUNK // HALF
N_BLOCK = TOTAL // HALF
STEPS = N_CHUNK + 1

SCALE = (D_NOPE + D_ROPE) ** (-0.5) * (0.1 * math.log(40.0) + 1.0) ** 2
LOG2E = math.log2(math.e)
HIDDEN = -1e30

GROUPS = [
    [c * N_HEAD + ((c // 8) ^ side) * 8 + z for c in range(core, N_CTX, 2)]
    for core in range(2)
    for side in range(2)
    for z in range(8)
]
ALONG_X = [(i, i ^ (8 * N_HEAD + 8)) for i in range(N_CTX * N_HEAD)]
ALONG_Y1 = [(c, c ^ 2) for c in range(N_CTX)]
ALONG_Y3 = [(c, c ^ 6) for c in range(N_CTX)]
OWNERS = (0, 2, 4, 6, 8, 10, 12, 14)
SWAP = [(c, c ^ 1) for c in range(N_CTX)]

AGAINST = (((1,), (1,)), ((), ()))

bf16 = jnp.bfloat16
f32 = jnp.float32


def frequencies():
    half = D_ROPE // 2
    index = np.arange(half, dtype=np.float64)
    width = 2 * half
    extra = np.power(10000.0, -2.0 * index / width)
    inter = extra / 40.0
    lower = math.floor(width * math.log(4096.0 / (32.0 * 2.0 * math.pi)) / (2.0 * math.log(10000.0)))
    upper = math.ceil(width * math.log(4096.0 / (1.0 * 2.0 * math.pi)) / (2.0 * math.log(10000.0)))
    lower = max(lower, 0)
    upper = min(upper, half - 1)
    spread = max(upper - lower, 0.001)
    ramp = np.clip((index - lower) / spread, 0.0, 1.0)
    inv = inter * ramp + extra * (1.0 - ramp)
    return np.tile(inv, 4).astype(np.float32)[None, :]


def split_half_pi():
    rest = math.pi / 2
    parts = []
    for bits in (9, 19):
        part = math.floor(rest * 2.0**bits) / 2.0**bits
        parts.append(part)
        rest -= part
    return parts + [rest]


HALF_PI = split_half_pi()


def cos_sin(angle):
    turns = jnp.floor(angle * (2.0 / math.pi) + 0.5)
    r = angle - turns * HALF_PI[0]
    r = r - turns * HALF_PI[1]
    r = r - turns * HALF_PI[2]
    r2 = r * r
    sine = r + r * r2 * (-1.0 / 6 + r2 * (1.0 / 120 + r2 * (-1.0 / 5040 + r2 * (1.0 / 362880))))
    cosine = 1.0 + r2 * (-0.5 + r2 * (1.0 / 24 + r2 * (-1.0 / 720 + r2 * (1.0 / 40320))))
    quarter = turns.astype(jnp.int32) & 3
    odd = (quarter & 1) == 1
    cos_out = jnp.where(odd, sine, cosine)
    sin_out = jnp.where(odd, cosine, sine)
    cos_out = jnp.where((quarter == 1) | (quarter == 2), -cos_out, cos_out)
    sin_out = jnp.where(quarter >= 2, -sin_out, sin_out)
    return cos_out, sin_out


def lanes_of(shape):
    return lax.broadcasted_iota(jnp.int32, shape, 1)


def swap_halves(x):
    return jnp.where((lanes_of(x.shape) & 63) < 32, pltpu.roll(x, 96, 1), pltpu.roll(x, 32, 1))


def pair_tile(first, second, half):
    low = lanes_of(first.shape) < HALF
    if half == 0:
        return jnp.where(low, first, pltpu.roll(second, HALF, 1))
    return jnp.where(low, pltpu.roll(first, HALF, 1), second)


def pack_rope(rope):
    low = lanes_of((16, 128)) < D_ROPE
    tiles = []
    for m in (0, 2):
        tiles.append(jnp.where(low, rope[16 * m:16 * m + 16], pltpu.roll(rope[16 * m + 16:16 * m + 32], D_ROPE, 1)))
    return jnp.concatenate(tiles, axis=1)


def unpack_rope(packed):
    low = lanes_of((16, 128)) < D_ROPE
    pieces = []
    for m in range(4):
        tile = packed[:, (m // 2) * 128:(m // 2 + 1) * 128]
        pieces.append(jnp.where(low, pltpu.roll(tile, D_ROPE, 1) if m % 2 else tile, 0.0))
    return jnp.concatenate(pieces, axis=0)


def share_kernel(rank_ref, pos_ref, inv_ref, comp_ref, tile, cos_ref, sin_ref):
    pos = jnp.broadcast_to(pos_ref[...].astype(f32), (ROWS, ROWS)).T
    cosine, sine = cos_sin(pos * inv_ref[...])
    sine = jnp.where((lanes_of(sine.shape) & 63) < 32, -sine, sine)
    for k in range(D_LAT // 128):
        piece = slice(k * 128, (k + 1) * 128)
        tile[:ROWS, piece] = comp_ref[piece, :].astype(f32).T.astype(bf16)
    x = comp_ref[D_LAT:, :].astype(f32)
    x = jnp.concatenate([x, x], axis=0).T
    rotated = x * cosine + pltpu.roll(x, 32, 1) * sine
    for j in range(2):
        tile[ROWS:, j * 256:(j + 1) * 256] = pack_rope(rotated[j * HALF:(j + 1) * HALF]).astype(bf16)
    cos_ref[...] = cosine
    sin_ref[...] = sine


def absorb_kernel(qn_ref, qr_ref, go_ref, uk_ref, uv_ref, cos_ref, sin_ref,
                  both_ref):
    for pair in range(2):
        x = qr_ref[:, pair * 128:(pair + 1) * 128].astype(f32)
        rotated = x * cos_ref[...] + swap_halves(x) * sin_ref[...]
        turned = pltpu.roll(rotated, HALF, 1)
        for h in (2 * pair, 2 * pair + 1):
            cols = slice(h * D_NOPE, (h + 1) * D_NOPE)
            q = lax.dot_general(qn_ref[:, cols], uk_ref[:, cols], AGAINST, preferred_element_type=f32)
            g = lax.dot_general(go_ref[:, cols], uv_ref[:, cols], AGAINST, preferred_element_type=f32)
            rope = jnp.where(lanes_of(x.shape) < D_ROPE, turned if h % 2 else rotated, 0.0)
            dst = slice(h * HALF, (h + 1) * HALF)
            for j in range(2):
                src = slice(j * HALF, (j + 1) * HALF)
                both_ref[j, 0, dst, :D_LAT] = (q[src] * SCALE).astype(bf16)
                both_ref[j, 0, dst, D_LAT:] = (rope[src] * SCALE).astype(bf16)
                both_ref[j, 1, dst, :D_LAT] = g[src].astype(bf16)
                both_ref[j, 1, dst, D_LAT:] = jnp.zeros((HALF, 128), bf16)


def step_places(bm_ref, rank):
    first, second = bm_ref[0, rank], bm_ref[1, rank]
    early = jnp.where(first < second, 0, 1)
    low, high = jnp.minimum(first, second), jnp.maximum(first, second)
    count = (low + PER_CHUNK) // PER_CHUNK
    places = [(True, early, 0, 1, low)]
    places += [(False, 1 - early, 0, 2, high), (False, 1 - early, 2, 2, high), (False, 1 - early, 4, 1, high)]
    for k in range(1, 4):
        is_early = k < count
        places.append((
            is_early,
            jnp.where(is_early, early, 1 - early),
            jnp.where(is_early, k, N_CHUNK - k),
            1,
            jnp.where(is_early, low, high),
        ))
    starts = [0, 1, 3, 5, 6, 7, 8]
    return [(slice(at * CHUNK, (at + place[3]) * CHUNK), *place) for at, place in zip(starts, places)]


def pick(flag, first, second):
    if flag is True:
        return first
    if flag is False:
        return second
    return jnp.where(flag, first, second)


def chunk_rows(c, n):
    return pl.ds(c * CHUNK if isinstance(c, int) else pl.multiple_of(c * CHUNK, CHUNK), n * CHUNK)


def attend_kernel(bm_ref, rank_ref, both, *refs):
    shares, refs = refs[:2 * N_CHIP], refs[2 * N_CHIP:]
    dmine_ref, dother_ref, ds, keys, probs, dprobs, tops, dlat, drope = refs
    rank = rank_ref[0]
    core = rank & 1
    places = step_places(bm_ref, rank)
    for i, ref in enumerate(shares):
        row = rank ^ (OWNERS[i % N_CHIP] ^ (i // N_CHIP))
        for j in range(2):
            rows = pl.ds(pl.multiple_of(bm_ref[j, row] * HALF, HALF), HALF)
            keys[rows, :D_LAT] = ref[j * HALF:(j + 1) * HALF, :]
            packed = ref[ROWS:, j * 256:(j + 1) * 256].astype(f32)
            keys[rows, D_LAT:] = unpack_rope(packed).astype(bf16)

    zero = jnp.zeros((1, LANES), f32)
    start = (jnp.full((1, LANES), HIDDEN, f32), zero, zero)
    state = {True: start, False: start}
    offset = lax.broadcasted_iota(jnp.int32, (CHUNK, LANES), 0) - (
        lax.broadcasted_iota(jnp.int32, (CHUNK, LANES), 1) & (HALF - 1)
    )
    for i, (at, is_early, j, c, n, block) in enumerate(places):
        rows = chunk_rows(c, n)
        top, total, weighted = (pick(is_early, a, b) for a, b in zip(state[True], state[False]))
        scores = lax.dot_general(keys[rows, :], both[j, :LANES, :], AGAINST, preferred_element_type=f32)
        dp = lax.dot_general(keys[rows, :D_LAT], both[j, LANES:, :D_LAT], AGAINST, preferred_element_type=f32)
        scores = scores * LOG2E
        if n == 1:
            scores = jnp.where(offset <= block * HALF - c * CHUNK, scores, HIDDEN)
        new_top = jnp.maximum(top, jnp.max(scores, axis=0, keepdims=True))
        e = jnp.exp2(scores - new_top)
        keep = jnp.exp2(top - new_top)
        probs[at] = e
        dprobs[at] = dp
        tops[i] = new_top
        new = (
            new_top,
            total * keep + jnp.sum(e, axis=0, keepdims=True),
            weighted * keep + jnp.sum(e * dp, axis=0, keepdims=True),
        )
        if is_early is not False:
            state[True] = tuple(pick(is_early, a, b) for a, b in zip(new, state[True]))
        if is_early is not True:
            state[False] = tuple(pick(is_early, b, a) for a, b in zip(new, state[False]))

    stats = {}
    for flag, (top, total, weighted) in state.items():
        inverse = 1.0 / total
        stats[flag] = (top, inverse, weighted * inverse)

    def change(i):
        at, is_early, j, c, n, block = places[i]
        top, inverse, delta = (pick(is_early, a, b) for a, b in zip(stats[True], stats[False]))
        p = probs[at] * (jnp.exp2(tops[i] - top) * inverse)
        d = (p * (dprobs[at] - delta)).astype(bf16)
        ds[at] = d
        pair = jnp.concatenate([d, p.astype(bf16)], axis=1)
        latent = jnp.dot(pair, both[j, :, :D_LAT], preferred_element_type=f32)
        rope = jnp.dot(d, both[j, :LANES, D_LAT:], preferred_element_type=f32)
        return [(latent[k * CHUNK:(k + 1) * CHUNK], rope[k * CHUNK:(k + 1) * CHUNK]) for k in range(n)]

    def put(c, parts):
        rows = slice(c * CHUNK, (c + 1) * CHUNK)
        dlat[rows, :D_LAT] = parts[0].astype(bf16)
        for i in range(PER_CHUNK):
            part = parts[1][i * HALF:(i + 1) * HALF]
            drope[(c * PER_CHUNK + i) * 16:(c * PER_CHUNK + i + 1) * 16, :] = pack_rope(part).astype(bf16)

    early = change(0)
    for k in range(1, 4):
        turn = change(3 + k)[0]
        is_early = places[3 + k][1]
        put(N_CHUNK - k, [jnp.where(is_early, 0.0, x) for x in turn])
        early.append([jnp.where(is_early, x, 0.0) for x in turn])
    late = change(1) + change(2) + change(3)
    for c in range(4):
        put(c, [x + y for x, y in zip(late[c], early[c])])
    put(4, late[4])
    for chip in range(N_CHIP):
        for k, ref in enumerate((dmine_ref, dother_ref)):
            row = 2 * chip + (core ^ k)
            for j in range(2):
                block = bm_ref[j, row]
                ref[chip, j * HALF:(j + 1) * HALF, :] = dlat[pl.ds(pl.multiple_of(block * HALF, HALF), HALF), :]
                ref[chip, ROWS:, j * 256:(j + 1) * 256] = drope[pl.ds(pl.multiple_of(block * 16, 16), 16), :]


def spill_kernel(ds, keys, ds_hbm, keys_hbm, sems):
    copies = [pltpu.make_async_copy(ds, ds_hbm, sems.at[0]), pltpu.make_async_copy(keys, keys_hbm, sems.at[1])]
    for copy in copies:
        copy.start()
    for copy in copies:
        copy.wait()


def queries_kernel(bm_ref, rank_ref, keys_hbm, ds_hbm, uk_hbm, cos_ref, sin_ref, gqn_ref, gqr_ref,
                   keys, ds, uk_ref, total, sems, ds_sems):
    first = pltpu.make_async_copy(keys_hbm, keys, sems.at[0])
    weights = pltpu.make_async_copy(uk_hbm, uk_ref, sems.at[1])
    places = step_places(bm_ref, rank_ref[0])
    moves = [pltpu.make_async_copy(ds_hbm.at[p[0]], ds.at[p[0]], ds_sems.at[i]) for i, p in enumerate(places)]
    first.start()
    for move in moves:
        move.start()
    weights.start()
    total[...] = jnp.zeros_like(total)
    first.wait()
    for move, (at, _, j, c, n, _) in zip(moves, places):
        move.wait()
        total[j] += lax.dot_general(
            ds[at], keys[chunk_rows(c, n), :], (((0,), (0,)), ((), ())), preferred_element_type=f32
        )
    weights.wait()
    for pair in range(HEADS // 2):
        ropes = []
        for h in (2 * pair, 2 * pair + 1):
            rows = slice(h * HALF, (h + 1) * HALF)
            both = jnp.concatenate([total[0, rows, :], total[1, rows, :]], axis=0) * SCALE
            cols = slice(h * D_NOPE, (h + 1) * D_NOPE)
            gqn_ref[:, cols] = jnp.dot(
                both[:, :D_LAT].astype(bf16), uk_ref[:, cols], preferred_element_type=f32
            ).astype(bf16)
            ropes.append(both[:, D_LAT:])
        g = jnp.where(lanes_of(ropes[0].shape) < D_ROPE, ropes[0], pltpu.roll(ropes[1], D_ROPE, 1))
        g = g * cos_ref[...] - swap_halves(g) * sin_ref[...]
        gqr_ref[:, pair * 128:(pair + 1) * 128] = g.astype(bf16)


def after_kernel(first_ref, second_ref, out_ref):
    pass


def pair_kernel(ours_ref, theirs_ref, later_ref, out_ref):
    for i in range(N_CHIP):
        out_ref[i] = (ours_ref[i].astype(f32) + theirs_ref[i].astype(f32)).astype(bf16)


def chips_kernel(parts_ref, cos_ref, sin_ref, later_ref, out_ref):
    total = parts_ref[0].astype(f32)
    for i in range(1, N_CHIP):
        total = total + parts_ref[i].astype(f32)
    out_ref[:, :D_LAT] = total[:ROWS].astype(bf16)
    g = jnp.concatenate([unpack_rope(total[ROWS:, j * 256:(j + 1) * 256]) for j in range(2)], axis=0)
    g = g * cos_ref[...] - swap_halves(g) * sin_ref[...]
    out_ref[:, D_LAT:] = g[:, :D_ROPE].astype(bf16)


def heads_kernel(parts_ref, out_ref):
    total = parts_ref[0].astype(f32)
    for i in range(1, N_HEAD):
        total = total + parts_ref[i].astype(f32)
    total = total.astype(bf16)
    for i in range(N_HEAD):
        out_ref[i] = total


def whole(count):
    return [pl.BlockSpec(memory_space=pltpu.VMEM)] * count


def in_hbm(x):
    return pltpu.with_memory_space_constraint(x, pltpu.HBM)


def params(mib):
    return pltpu.CompilerParams(vmem_limit_bytes=mib * 1024 * 1024)


ANY = pl.BlockSpec(memory_space=pl.ANY)
HBM = pl.BlockSpec(memory_space=pltpu.HBM)
ALL_MIB = 60

SMEM = pl.BlockSpec(memory_space=pltpu.SMEM)


def attend_call(*operands):
    shape = jax.ShapeDtypeStruct
    piece = shape((N_CHIP, PACKED, D_LAT), bf16)
    return pl.pallas_call(
        attend_kernel,
        in_specs=[SMEM, SMEM] + whole(1 + 2 * N_CHIP),
        out_specs=tuple(whole(4)),
        out_shape=(piece, piece, shape((STEPS * CHUNK, LANES), bf16), shape((TOTAL, D_PAD), bf16)),
        scratch_shapes=[
            pltpu.VMEM((STEPS * CHUNK, LANES), f32),
            pltpu.VMEM((STEPS * CHUNK, LANES), f32),
            pltpu.VMEM((STEPS, 1, LANES), f32),
            pltpu.VMEM((TOTAL, D_LAT), bf16),
            pltpu.VMEM((N_BLOCK * 16, 256), bf16),
        ],
        compiler_params=params(36),
        name="attend",
    )(*operands)


def on_device(q_nope, q_rope, compressed, w_uk, w_uv, grad_out, positions, block_map):
    rank = lax.axis_index("ctx").astype(jnp.int32).reshape(1)
    blocks = block_map.T
    shape = jax.ShapeDtypeStruct
    table = shape((ROWS, 128), f32)
    shared, cosine, sine = pl.pallas_call(
        share_kernel,
        in_specs=[SMEM] + whole(3),
        out_specs=tuple(whole(3)),
        out_shape=(shape((PACKED, D_LAT), bf16), table, table),
        compiler_params=params(ALL_MIB),
        name="share",
    )(rank, positions.reshape(1, ROWS), jnp.asarray(frequencies()), compressed.T)
    x = lambda a: lax.ppermute(a, ("ctx", "head"), ALONG_X)
    y1 = lambda a: lax.ppermute(a, "ctx", ALONG_Y1)
    y3 = lambda a: lax.ppermute(a, "ctx", ALONG_Y3)
    swap = lambda a: lax.ppermute(a, "ctx", SWAP)
    held = {0: shared, 8: x(shared), 2: y1(shared), 6: y3(shared)}
    held.update({10: y1(held[8]), 4: y3(held[2]), 14: x(held[6])})
    pair_cols = lambda width: pl.BlockSpec((ROWS, width), lambda p: (0, p))
    fixed = pl.BlockSpec((ROWS, 128), lambda p: (0, 0))
    weight = pl.BlockSpec((D_LAT, 512), lambda p: (0, p))
    both = pl.pallas_call(
        absorb_kernel,
        grid=(HEADS // 4,),
        in_specs=[pair_cols(512), pair_cols(256), pair_cols(512), weight, weight, fixed, fixed],
        out_specs=pl.BlockSpec((2, 2, 256, D_PAD), lambda p: (0, 0, p, 0)),
        out_shape=shape((2, 2, LANES, D_PAD), bf16),
        compiler_params=params(16),
        cost_estimate=pl.CostEstimate(flops=300_000_000, bytes_accessed=8_000_000, transcendentals=0),
        name="absorb",
    )(*map(in_hbm, (q_nope, q_rope, grad_out, w_uk, w_uv, cosine, sine)))

    held[4] = pl.pallas_call(
        after_kernel,
        in_specs=[ANY, ANY],
        out_specs=ANY,
        out_shape=shape((PACKED, D_LAT), bf16),
        input_output_aliases={0: 0},
        compiler_params=params(8),
        name="after",
    )(held[4], both)
    held[12] = x(held[4])
    mine = [held[owner] for owner in OWNERS]
    other = [swap(share) for share in mine]
    both = both.reshape(2, 2 * LANES, D_PAD)
    dmine, dother, ds, keys = attend_call(blocks, rank, both, *mine, *other)
    ds, keys = pl.pallas_call(
        spill_kernel,
        in_specs=[ANY, ANY],
        out_specs=(HBM, HBM),
        out_shape=(pltpu.HBM(ds.shape, bf16), pltpu.HBM(keys.shape, bf16)),
        scratch_shapes=[pltpu.SemaphoreType.DMA((2,))],
        compiler_params=params(8),
        cost_estimate=pl.CostEstimate(flops=0, bytes_accessed=10_000_000, transcendentals=0),
        name="spill",
    )(ds, keys)

    theirs = lax.ppermute(dother, "ctx", SWAP)
    summed = pl.pallas_call(
        pair_kernel,
        in_specs=whole(2) + [HBM],
        out_specs=whole(1)[0],
        out_shape=shape(dmine.shape, bf16),
        compiler_params=params(16),
        name="pair",
    )(dmine, theirs, in_hbm(ds))
    parts = lax.all_to_all(summed, ("ctx", "head"), 0, 0, axis_index_groups=GROUPS)

    grad_q_nope, grad_q_rope = pl.pallas_call(
        queries_kernel,
        in_specs=[SMEM, SMEM, HBM, HBM, HBM] + whole(2),
        out_specs=tuple(whole(2)),
        out_shape=(shape((ROWS, HEADS * D_NOPE), bf16), shape((ROWS, HEADS * D_ROPE), bf16)),
        scratch_shapes=[
            pltpu.VMEM((TOTAL, D_PAD), bf16),
            pltpu.VMEM((STEPS * CHUNK, LANES), bf16),
            pltpu.VMEM((D_LAT, HEADS * D_NOPE), bf16),
            pltpu.VMEM((2, LANES, D_PAD), f32),
            pltpu.SemaphoreType.DMA((2,)),
            pltpu.SemaphoreType.DMA((STEPS,)),
        ],
        compiler_params=params(ALL_MIB),
        cost_estimate=pl.CostEstimate(flops=4_000_000_000, bytes_accessed=9_000_000, transcendentals=0),
        name="queries",
    )(blocks, rank, in_hbm(keys), in_hbm(ds), in_hbm(w_uk), cosine, sine)

    owned = pl.pallas_call(
        chips_kernel,
        in_specs=whole(3) + [HBM],
        out_specs=whole(1)[0],
        out_shape=shape((ROWS, D_ALL), bf16),
        compiler_params=params(16),
        name="chips",
    )(parts, cosine, sine, in_hbm(grad_q_rope))
    slabs = lax.all_to_all(owned.reshape(N_HEAD, ROWS // N_HEAD, D_ALL), "head", 0, 0)
    slabs = pl.pallas_call(
        heads_kernel,
        in_specs=whole(1),
        out_specs=whole(1)[0],
        out_shape=shape((N_HEAD, ROWS // N_HEAD, D_ALL), bf16),
        compiler_params=params(16),
        name="heads",
    )(slabs)
    grad_compressed = lax.all_to_all(slabs, "head", 0, 0).reshape(ROWS, D_ALL)
    return grad_q_nope, grad_q_rope, grad_compressed


def solution(mesh):
    in_specs = (
        P("ctx", "head"),
        P("ctx", "head"),
        P("ctx", None),
        P(None, "head"),
        P(None, "head"),
        P("ctx", "head"),
        P("ctx"),
        P(),
    )
    out_specs = (P("ctx", "head"), P("ctx", "head"), P("ctx", None))
    return jax.shard_map(
        on_device, mesh=mesh, in_specs=in_specs, out_specs=out_specs, check_vma=False
    )
```
